32 devices in a mesh: det: 4 (over y, x), tm: 8 (over z, core).
Axes of the slice: x: 2, y: 2, z: 4, core: 2. Of those that a mesh axis runs over, the one named last changes fastest.
Arguments:
- detector_data: float32 [128, 65536], P('det', 'tm'), may hold values from -250 to 250
- templates: bfloat16 [8, 16, 65536], P(None, None, 'tm'), may hold values from -5 to 5
- wafer_of: int32 [128], P('det'), may hold values from 0 to 7, as said below
- knee_freq: float32 [128], P(('det', 'tm')), may hold values from 0.1 to 5
- white_level: float32 [128], P(('det', 'tm')), may hold values from 0.5 to 5
- tile_id: int32 [128, 65536], P(('det', 'tm')), may hold values from 0 to 15
- pixel_id: int32 [128, 65536], P(('det', 'tm')), may hold values from 0 to 127
- tile_order: int32 [16], replicated, may hold values from 0 to 15, each once
Outputs:
- fit_amps: float32 [16, 128], P(None, 'det')
- weighted_data: bfloat16 [128, 65536], P(('det', 'tm'))
- sky_map: float32 [2048], P('tm')
- weight_map: float32 [2048], P('tm')
The draws below stay inside these ranges and needn't reach their ends.
Inputs may be any that keep to these rules, and one draw needn't show every extreme that they name: `wafer_of`: the detectors of each aligned run of 16 share one wafer, and each wafer has exactly one such run.
All inputs are finite; a program needn't handle non-finite values.
Results may differ from the reference program's by a relative error of at most 0.0016.
Values sent between devices are 32-bit elements; how exact they have to be, the bound alone decides.
No kernel may reach another device: no remote copies, remote signals or barrier semaphores. Data moves between devices by JAX's collectives and lax.ppermute only.
A program may use at most 64 MiB of HBM per device.

```python
import math
import jax
import jax.numpy as jnp
from jax import lax

SAMPLES = 65536
WAFERS = 8
MODES = 16
TILES = 16
PIX = 128
DETS = 128


def shared_fields(key):
    base_key = jax.random.fold_in(key, 4242)
    subkeys = jax.random.split(base_key, 12)
    wafer_label = jax.random.permutation(subkeys[0], WAFERS).astype(jnp.int32)
    run_index = (jnp.arange(DETS, dtype=jnp.int32) // (DETS // WAFERS)).astype(jnp.int32)
    wafer_of = wafer_label[run_index]
    first_rank = jax.random.randint(subkeys[1], (DETS, SAMPLES), 0, TILES, dtype=jnp.int32)
    second_rank = jax.random.randint(subkeys[2], (DETS, SAMPLES), 0, TILES, dtype=jnp.int32)
    tile_label = jax.random.permutation(subkeys[3], TILES).astype(jnp.int32)
    tile_id = tile_label[jnp.minimum(first_rank, second_rank)]
    pixel_id = jax.random.randint(subkeys[4], (DETS, SAMPLES), 0, PIX, dtype=jnp.int32)
    return (wafer_of, tile_id, pixel_id, subkeys)


def template_values(subkeys):
    raw_values = jax.random.normal(subkeys[5], (WAFERS, MODES, SAMPLES), jnp.float32)
    return jnp.clip(raw_values, -5.0, 5.0)


def draw_templates(key, part):
    wafer_of, tile_id, pixel_id, subkeys = shared_fields(key)
    return template_values(subkeys).astype(jnp.bfloat16)


def draw_wafer_of(key, part):
    wafer_of, tile_id, pixel_id, subkeys = shared_fields(key)
    return wafer_of


def draw_tile_id(key, part):
    wafer_of, tile_id, pixel_id, subkeys = shared_fields(key)
    return tile_id


def draw_pixel_id(key, part):
    wafer_of, tile_id, pixel_id, subkeys = shared_fields(key)
    return pixel_id


def draw_detector_data(key, part):
    wafer_of, tile_id, pixel_id, subkeys = shared_fields(key)
    rounded = template_values(subkeys).astype(jnp.bfloat16).astype(jnp.float32)
    amplitude = jax.random.uniform(subkeys[7], (DETS, MODES), jnp.float32, -3.0, 3.0)
    wafer_hot = (wafer_of[:, None] == jnp.arange(WAFERS, dtype=jnp.int32)[None, :]).astype(jnp.float32)
    coefficients = (wafer_hot[:, :, None] * amplitude[:, None, :]).reshape(DETS, WAFERS * MODES)
    common_part = jnp.dot(coefficients, rounded.reshape(WAFERS * MODES, SAMPLES))
    sky_truth = jax.random.uniform(subkeys[8], (TILES, PIX), jnp.float32, -2.0, 2.0)
    sky_part = sky_truth[tile_id, pixel_id]
    noise_part = jnp.clip(jax.random.normal(subkeys[11], (DETS, SAMPLES), jnp.float32), -6.0, 6.0)
    return (common_part + sky_part + noise_part).astype(jnp.float32)


def level_of(key, extent, cuts, low, largest):
    factor_of = 1.0
    for position, blocks in cuts:
        steps = jax.random.uniform(jax.random.fold_in(jax.random.fold_in(key, 6), position), (blocks,), jnp.float32, low / len(cuts), largest / len(cuts))
        factor_of = factor_of * jnp.repeat(jnp.exp(steps), extent[position] // blocks).reshape((-1,) + (1,) * (len(extent) - 1 - position))
    return factor_of


def setup_inputs(seed: int = 0) -> dict:
    seeds = jax.random.split(jax.random.key(seed), 9)
    detector_data = draw_detector_data(jax.random.fold_in(seeds[8], 71), 0)
    templates = draw_templates(jax.random.fold_in(seeds[8], 71), 0)
    wafer_of = draw_wafer_of(jax.random.fold_in(seeds[8], 71), 0)
    knee_freq = jnp.clip(jnp.exp(math.log(5.0) - 3.912023 * jax.random.uniform(seeds[3], (DETS,), jnp.float32) ** level_of(seeds[3], (DETS,), ((0, 32),), -0.2, 0.2)), 0.1, 5.0)
    white_level = jnp.clip(jnp.exp(math.log(5.0) - 2.3025851 * jax.random.uniform(seeds[4], (DETS,), jnp.float32) ** level_of(seeds[4], (DETS,), ((0, 32),), -0.2, 0.2)), 0.5, 5.0)
    tile_id = draw_tile_id(jax.random.fold_in(seeds[8], 71), 0)
    pixel_id = draw_pixel_id(jax.random.fold_in(seeds[8], 71), 0)
    tile_order = jax.random.permutation(seeds[7], TILES).astype(jnp.int32)
    return dict(detector_data=detector_data, templates=templates, wafer_of=wafer_of, knee_freq=knee_freq, white_level=white_level, tile_id=tile_id, pixel_id=pixel_id, tile_order=tile_order)


precise = lax.Precision.HIGHEST
sample_rate = 200.0


def invert_blocks(matrices):
    dimension = matrices.shape[-1]
    identity = jnp.broadcast_to(jnp.eye(dimension, dtype=matrices.dtype), matrices.shape)
    joined = jnp.concatenate([matrices, identity], axis=-1)
    for column in range(dimension):
        pivot_row = joined[:, column, :] / joined[:, column, column][:, None]
        factor = joined[:, :, column]
        joined = joined - factor[:, :, None] * pivot_row[:, None, :]
        joined = joined.at[:, column, :].set(pivot_row)
    return joined[:, :, dimension:]


def spectral_weight(frequency, knee_rows, white_rows):
    squared = frequency * frequency
    return squared[None, :] / (white_rows[:, None] * (squared[None, :] + knee_rows[:, None] ** 2))


def reference(detector_data, templates, wafer_of, knee_freq, white_level, tile_id, pixel_id, tile_order):
    wafer_count = templates.shape[0]
    mode_count = templates.shape[1]
    full_length = templates.shape[2]
    detector_count = detector_data.shape[0]
    wide_templates = templates.astype(jnp.float32)
    flat_templates = wide_templates.reshape(wafer_count * mode_count, full_length)
    gram_matrix = jnp.einsum('wkt,wjt->wkj', wide_templates, wide_templates, precision=precise)
    inverse_gram = invert_blocks(gram_matrix)
    block_rows = math.gcd(detector_count, 64)
    block_count = detector_count // block_rows
    wafer_ramp = jnp.arange(wafer_count, dtype=jnp.int32)
    bin_index = jnp.arange(full_length // 2 + 1).astype(jnp.float32)
    frequency = bin_index * (sample_rate / full_length)
    cell_total = TILES * PIX

    def one_block(totals, inputs):
        data_rows, wafer_rows, knee_rows, white_rows, tile_rows, pixel_rows = inputs
        wafer_hot = (wafer_rows[None, :] == wafer_ramp[:, None]).astype(jnp.float32)
        projected = jnp.einsum('ct,bt->cb', flat_templates, data_rows, precision=precise)
        projected = projected.reshape(wafer_count, mode_count, block_rows)
        solved = jnp.einsum('wkj,wjb->wkb', inverse_gram, projected, precision=precise)
        amps_rows = jnp.einsum('wkb,wb->kb', solved, wafer_hot, precision=precise)
        coefficients = (wafer_hot[:, None, :] * amps_rows[None, :, :]).reshape(wafer_count * mode_count, block_rows)
        fitted = jnp.einsum('cb,ct->bt', coefficients, flat_templates, precision=precise)
        residual = data_rows - fitted
        spectrum = jnp.fft.rfft(residual, axis=-1)
        filtered = jnp.fft.irfft(spectrum * spectral_weight(frequency, knee_rows, white_rows), n=full_length, axis=-1)
        weighted_rows = filtered.astype(jnp.float32).astype(jnp.bfloat16)
        inverse_white = (1.0 / white_rows).astype(jnp.bfloat16)
        cell_rows = (tile_rows * PIX + pixel_rows).reshape(-1).astype(jnp.int32)
        values = lax.optimization_barrier(weighted_rows).astype(jnp.float32).reshape(-1)
        white_wide = lax.optimization_barrier(inverse_white).astype(jnp.float32)
        weights = jnp.broadcast_to(white_wide[:, None], tile_rows.shape).reshape(-1)
        sky_part = jax.ops.segment_sum(values, cell_rows, num_segments=cell_total)
        weight_part = jax.ops.segment_sum(weights, cell_rows, num_segments=cell_total)
        return (totals[0] + sky_part, totals[1] + weight_part), (amps_rows, weighted_rows)

    inputs = (
        detector_data.reshape(block_count, block_rows, full_length),
        wafer_of.reshape(block_count, block_rows),
        knee_freq.reshape(block_count, block_rows),
        white_level.reshape(block_count, block_rows),
        tile_id.reshape(block_count, block_rows, full_length),
        pixel_id.reshape(block_count, block_rows, full_length),
    )
    start_totals = (jnp.zeros((cell_total,), jnp.float32), jnp.zeros((cell_total,), jnp.float32))
    totals, outputs = lax.scan(one_block, start_totals, inputs)
    amps_blocks, weighted_blocks = outputs
    fit_amps = jnp.transpose(amps_blocks, (1, 0, 2)).reshape(mode_count, detector_count)
    weighted_data = weighted_blocks.reshape(detector_count, full_length)
    scale = float(TILES * PIX) / float(detector_count * full_length)
    sky_map = totals[0].reshape(TILES, PIX)[tile_order].reshape(-1) * scale
    weight_map = totals[1].reshape(TILES, PIX)[tile_order].reshape(-1) * scale
    return fit_amps, weighted_data, sky_map, weight_map
```

```python
import functools
import math

import jax
import jax.numpy as jnp
import numpy as np
from jax import lax
from jax.experimental import pallas as pl
from jax.experimental.pallas import tpu as pltpu
from jax.sharding import PartitionSpec as P

PIX = 128
COLS = 256
LANES = 128
HALVES = COLS // LANES
LOW = 64
SAMPLE_RATE = 200.0
MIB = 1024 * 1024
NT = (((1,), (1,)), ((), ()))
f32 = jnp.float32
bf16 = jnp.bfloat16


def split2(x):
    high = x.astype(bf16)
    return high, (x - high.astype(f32)).astype(bf16)


def split3(x):
    high = x.astype(bf16)
    rest = x - high.astype(f32)
    mid = rest.astype(bf16)
    return high, mid, (rest - mid.astype(f32)).astype(bf16)


def host_split(x):
    high = x.astype(np.float32).astype(bf16)
    low = (x - high.astype(np.float64)).astype(np.float32).astype(bf16)
    return high, low


@functools.lru_cache(maxsize=None)
def tables(rows):
    total = rows * COLS
    half = rows // 2
    slots = np.arange(half)
    slots[0] = half
    ramp = np.arange(rows)
    angle = 2.0 * np.pi * (slots[:, None] * ramp[None, :] % rows) / rows
    first = np.concatenate([np.cos(angle), -np.sin(angle)], axis=0)
    first[half] = 1.0
    weight = np.full((half,), 2.0)
    weight[0] = 1.0
    last = np.concatenate([weight[:, None] * np.cos(angle), -2.0 * np.sin(angle)], axis=0)
    last[half] = 1.0
    last = last.T / total
    col = np.arange(COLS)
    phase = 2.0 * np.pi * (col[:, None] * col[None, :] % COLS) / COLS
    side = np.concatenate([np.cos(phase), np.sin(phase)], axis=1)
    turn = 2.0 * np.pi * (slots[:, None] * col[None, :] % total) / total
    bins = np.concatenate([slots, np.zeros((16,), np.int64)])[:, None] + rows * col[None, :]
    freq = np.minimum(bins, total - bins).astype(np.float32) * np.float32(SAMPLE_RATE / total)
    return (
        *host_split(first),
        *host_split(side),
        *host_split(last),
        np.cos(turn).astype(np.float32),
        np.sin(turn).astype(np.float32),
        (freq * freq).astype(np.float32),
    )


def dot3(left, right, lhs_const):
    (lh, ll), (rh, rl) = left, right
    return jnp.dot(
        jnp.concatenate([lh, ll, lh], axis=1),
        jnp.concatenate([rh, rh, rl], axis=0),
        preferred_element_type=f32,
    )


def fit_kernel(runs, run_len, wafer_ref, *refs):
    data_ref, template_refs, out_ref = refs[0], refs[1:-1], refs[-1]
    parts = []
    for run in range(runs):
        temp = template_refs[run][0]
        modes = temp.shape[0]
        high, mid, low = split3(data_ref[run * run_len : (run + 1) * run_len, :])
        both = lax.dot_general(
            temp, jnp.concatenate([temp, high, mid, low], axis=0), NT, preferred_element_type=f32
        )
        ends = [modes + i * run_len for i in range(4)]
        parts.append(both[:, :modes])
        parts.append(
            both[:, ends[0] : ends[1]] + both[:, ends[1] : ends[2]] + both[:, ends[2] : ends[3]]
        )
    part = jnp.concatenate(parts, axis=1)

    @pl.when(pl.program_id(0) == 0)
    def _():
        out_ref[...] = part

    @pl.when(pl.program_id(0) > 0)
    def _():
        out_ref[...] += part


def residual_kernel(runs, run_len, owners, split_out, scalar_ref, sums_ref, data_ref, *refs):
    template_refs = refs[:runs]
    amps_ref, out_refs, rows_ref = refs[runs], refs[runs + 1 : -1], refs[-1]
    modes = template_refs[0].shape[1]
    row_count, time_local = data_ref.shape
    pieces = time_local // COLS
    width = modes + run_len
    row_index = lax.broadcasted_iota(jnp.int32, (modes, width), 0)
    joined = [sums_ref[:, run * width : (run + 1) * width] for run in range(runs)]
    for column in range(modes):
        for run in range(runs):
            now = joined[run]
            pivot_row = now[column : column + 1, :] / now[column : column + 1, column : column + 1]
            rest = now - now[:, column : column + 1] * pivot_row
            joined[run] = jnp.where(row_index == column, pivot_row, rest)
    amps = [now[:, modes:] for now in joined]
    amps_ref[...] = jnp.concatenate(amps, axis=1)
    for run in range(runs):
        temp = template_refs[run][0]
        left = jnp.concatenate(split3(amps[run].T), axis=1)
        fitted = jnp.dot(left, jnp.concatenate([temp] * 3, axis=0), preferred_element_type=f32)
        rows = slice(run * run_len, (run + 1) * run_len)
        for lane in range(time_local // LANES):
            cols = slice(lane * LANES, (lane + 1) * LANES)
            start = (lane % HALVES * pieces + lane // HALVES) * row_count + run * run_len
            rows_ref[start : start + run_len, :] = data_ref[rows, cols] - fitted[:, cols]
    local_dets = row_count // owners
    me = scalar_ref[row_count]
    for step in range(owners):
        owner = jnp.bitwise_xor(me, step) if split_out else step
        for det in range(local_dets):
            block = take_rows(rows_ref, owner * local_dets + det, pieces, row_count)
            if split_out:
                out_refs[step][det] = block
            else:
                out_refs[0][step, det] = block


def take_rows(ref, start, count, stride):
    return jnp.concatenate(
        [
            ref[pl.ds(side * count * stride + start, count, stride=stride), :]
            for side in range(HALVES)
        ],
        axis=1,
    )


def one_hot_pair(high_rows, low_rows, value_rows, tall):
    high_ramp = lax.broadcasted_iota(jnp.int32, (tall, COLS), 0).astype(f32).astype(bf16)
    low_ramp = lax.broadcasted_iota(jnp.int32, (LOW, COLS), 0).astype(f32).astype(bf16)
    lefts, rights = [], []
    for row in range(high_rows.shape[0]):
        high = jnp.broadcast_to(high_rows[row : row + 1], (tall, COLS)).astype(bf16)
        low = jnp.broadcast_to(low_rows[row : row + 1], (LOW, COLS)).astype(bf16)
        if value_rows.shape[0] == 1:
            value = jnp.broadcast_to(value_rows, (tall, COLS)).astype(bf16)
        else:
            value = jnp.broadcast_to(value_rows[row : row + 1], (tall, COLS)).astype(bf16)
        lefts.append(jnp.where(high == high_ramp, value, jnp.zeros_like(value)))
        rights.append(jnp.where(low == low_ramp, jnp.ones_like(low), jnp.zeros_like(low)))
    return lax.dot_general(
        jnp.concatenate(lefts, axis=1),
        jnp.concatenate(rights, axis=1),
        NT,
        preferred_element_type=f32,
    )


def weight_kernel(tall, white_ref, after_ref, tile_ref, pixel_ref, high_ref, low_ref, out_ref, hi_s, lo_s):
    local_dets, rows = high_ref.shape[0], high_ref.shape[1]
    cell = tile_ref[...] * PIX + pixel_ref[...]
    high = jnp.right_shift(cell, LOW.bit_length() - 1).astype(f32)
    low = jnp.bitwise_and(cell, LOW - 1).astype(f32)
    for lane in range(rows * HALVES):
        cols = slice(lane * LANES, (lane + 1) * LANES)
        start = (lane % HALVES * rows + lane // HALVES) * local_dets
        hi_s[start : start + local_dets, :] = high[:, cols]
        lo_s[start : start + local_dets, :] = low[:, cols]
    for det in range(local_dets):
        high_ref[det] = take_rows(hi_s, det, rows, local_dets)
        low_ref[det] = take_rows(lo_s, det, rows, local_dets)
    out_ref[...] = jnp.zeros_like(out_ref)
    chunk = min(64, rows)

    @pl.loop(0, local_dets)
    def _(det):
        value = jnp.full((1, COLS), white_ref[det], f32)

        @pl.loop(0, rows // chunk)
        def _(turn):
            here = pl.ds(pl.multiple_of(turn * chunk, chunk), chunk)
            out_ref[...] += one_hot_pair(high_ref[det, here], low_ref[det, here], value, tall)


def filter_kernel(parts, place_ref, order_ref, knee_ref, white_ref, *refs):
    part_refs = refs[:parts]
    (high_ref, low_ref, wsum_ref, f_h, f_l, s_h, s_l, l_h, l_l, tc_ref, ts_ref, sq_ref) = refs[
        parts : parts + 12
    ]
    out_ref, sky_ref, weight_ref, signal, stacked, totals = refs[parts + 12 :]
    det = pl.program_id(0)
    local_dets = pl.num_programs(0)
    dets = out_ref.shape[0]
    rows = signal.shape[0]
    half = rows // 2
    for part in range(parts):
        height = part_refs[part].shape[1]
        start = place_ref[part] * height if parts > 1 else 0
        if parts > 1:
            start = pl.multiple_of(start, height)
        signal[pl.ds(start, height), :] = part_refs[part][0]
    row_index = lax.broadcasted_iota(jnp.int32, (half, COLS), 0)
    turn_cos, turn_sin = tc_ref[...], ts_ref[...]
    side = (s_h[...], s_l[...])
    first = dot3((f_h[...], f_l[...]), split2(signal[...]), True)
    real_y, low_y = first[:half], first[half:]
    imag_y = jnp.where(row_index == 0, 0.0, low_y)
    zero_y = jnp.broadcast_to(low_y[0:1], (16, COLS))
    real_z = real_y * turn_cos + imag_y * turn_sin
    imag_z = imag_y * turn_cos - real_y * turn_sin
    forward = dot3(split2(jnp.concatenate([real_z, imag_z, zero_y], axis=0)), side, False)
    cos_f, sin_f = forward[:, :COLS], forward[:, COLS:]
    squared = sq_ref[...]
    knee = knee_ref[det]
    gain = squared / (white_ref[det] * (squared + knee * knee))
    gain_main, gain_zero = gain[:half], gain[half:]
    real_x = (cos_f[:half] + sin_f[half : 2 * half]) * gain_main
    imag_x = (cos_f[half : 2 * half] - sin_f[:half]) * gain_main
    zero_r = cos_f[2 * half :] * gain_zero
    zero_i = -sin_f[2 * half :] * gain_zero
    back = dot3(split2(jnp.concatenate([real_x, imag_x, zero_r, zero_i], axis=0)), side, False)
    cos_b, sin_b = back[:, :COLS], back[:, COLS:]
    real_u = cos_b[:half] - sin_b[half : 2 * half]
    imag_u = sin_b[:half] + cos_b[half : 2 * half]
    zero_o = cos_b[2 * half : 2 * half + 16] - sin_b[2 * half + 16 :]
    real_v = real_u * turn_cos - imag_u * turn_sin
    imag_v = real_u * turn_sin + imag_u * turn_cos
    imag_v = jnp.where(row_index == 0, zero_o[0:1], imag_v)
    result = dot3((l_h[...], l_l[...]), split2(jnp.concatenate([real_v, imag_v], axis=0)), True)
    signal[...] = result
    for side_half in range(HALVES):
        cols = slice(side_half * LANES, (side_half + 1) * LANES)
        stacked[pl.ds(side_half * rows * dets + det, rows, stride=dets), :] = result[:, cols]

    @pl.when(det == 0)
    def _():
        totals[...] = jnp.zeros_like(totals)

    chunk = min(64, rows)

    @pl.loop(0, rows // chunk)
    def _(turn):
        here = pl.ds(pl.multiple_of(turn * chunk, chunk), chunk)
        totals[...] += one_hot_pair(
            high_ref[0, here], low_ref[0, here], signal[here, :], totals.shape[0]
        )

    @pl.when(det == local_dets - 1)
    def _():
        for lane in range(rows * HALVES):
            start = (lane % HALVES * rows + lane // HALVES) * dets
            out_ref[:, lane * LANES : (lane + 1) * LANES] = stacked[
                start : start + dets, :
            ].astype(bf16)
        per_tile = PIX // LOW
        for tile in range(sky_ref.shape[0]):
            source = order_ref[tile] * per_tile
            for piece in range(per_tile):
                cols = slice(piece * LOW, (piece + 1) * LOW)
                sky_ref[tile : tile + 1, cols] = totals[pl.ds(source + piece, 1), :]
                weight_ref[tile : tile + 1, cols] = wsum_ref[pl.ds(source + piece, 1), :]


def swap(x, step, axis):
    size = lax.axis_size(axis)
    return lax.ppermute(x, axis, [(i, i ^ step) for i in range(size)])


def vmem(limit):
    return pltpu.CompilerParams(vmem_limit_bytes=limit * MIB)


def shards(
    detector_data, templates, wafer_of, knee_freq, white_level, tile_id, pixel_id, tile_order
):
    row_count, time_local = detector_data.shape
    wafer_count, modes, _ = templates.shape
    owners, groups = lax.axis_size("tm"), lax.axis_size("det")
    run_len = min(row_count, row_count * groups // wafer_count)
    runs = row_count // run_len
    width = runs * (modes + run_len)
    local_dets = row_count // owners
    full_length = time_local * owners
    rows = full_length // COLS
    pieces = time_local // COLS
    me = lax.axis_index("tm").astype(jnp.int32)
    power = owners & (owners - 1) == 0

    step_len = min(2048, time_local)

    def template_spec(run, blocked):
        length = step_len if blocked else time_local
        return pl.BlockSpec(
            (1, modes, length),
            lambda i, w, run=run: (w[run * run_len], 0, i if blocked else 0),
        )

    sums = pl.pallas_call(
        functools.partial(fit_kernel, runs, run_len),
        out_shape=jax.ShapeDtypeStruct((modes, width), f32),
        grid_spec=pltpu.PrefetchScalarGridSpec(
            num_scalar_prefetch=1,
            grid=(time_local // step_len,),
            in_specs=[pl.BlockSpec((row_count, step_len), lambda i, w: (0, i))]
            + [template_spec(run, True) for run in range(runs)],
            out_specs=pl.BlockSpec((modes, width), lambda i, w: (0, 0)),
        ),
        compiler_params=vmem(24),
        name="fit_sums",
    )(wafer_of, detector_data, *[templates] * runs)
    if power:
        step = 1
        while step < owners:
            sums = sums + swap(sums, step, "tm")
            step *= 2
    else:
        sums = lax.psum(sums, "tm")

    split_out = power and owners <= 8
    block_shape = (local_dets, pieces, COLS)
    if split_out:
        out_blocks = [jax.ShapeDtypeStruct(block_shape, f32)] * owners
        block_specs = [pl.BlockSpec(block_shape, lambda i, w: (0, 0, 0))] * owners
    else:
        out_blocks = [jax.ShapeDtypeStruct((owners, *block_shape), f32)]
        block_specs = [pl.BlockSpec((owners, *block_shape), lambda i, w: (0, 0, 0, 0))]
    fit_amps, *blocks = pl.pallas_call(
        functools.partial(residual_kernel, runs, run_len, owners, split_out),
        out_shape=[jax.ShapeDtypeStruct((modes, row_count), f32), *out_blocks],
        grid_spec=pltpu.PrefetchScalarGridSpec(
            num_scalar_prefetch=1,
            grid=(1,),
            in_specs=[
                pl.BlockSpec((modes, width), lambda i, w: (0, 0)),
                pl.BlockSpec((row_count, time_local), lambda i, w: (0, 0)),
            ]
            + [template_spec(run, False) for run in range(runs)],
            out_specs=[pl.BlockSpec((modes, row_count), lambda i, w: (0, 0)), *block_specs],
            scratch_shapes=[pltpu.VMEM((HALVES * pieces * row_count, LANES), f32)],
        ),
        compiler_params=vmem(32),
        name="residual",
    )(jnp.concatenate([wafer_of, me[None]]), sums, detector_data, *[templates] * runs)

    if split_out:
        received = [blocks[0]] + [None] * (owners - 1)
        for step in reversed(range(1, owners)):
            received[step] = swap(blocks[step], step, "tm")
        place = jnp.bitwise_xor(me, jnp.arange(owners, dtype=jnp.int32))
    else:
        moved = lax.all_to_all(blocks[0], "tm", split_axis=0, concat_axis=0, tiled=True)
        received = [jnp.swapaxes(moved, 0, 1).reshape(local_dets, rows, COLS)]
        place = jnp.zeros((1,), jnp.int32)

    tile_count = tile_order.shape[0]
    tall = tile_count * PIX // LOW
    inverse_white = (1.0 / white_level).astype(bf16).astype(f32)
    smem = pl.BlockSpec(memory_space=pltpu.SMEM)
    whole = pl.BlockSpec(memory_space=pltpu.VMEM)
    cells = local_dets * full_length
    high, low, weight_sum = pl.pallas_call(
        functools.partial(weight_kernel, tall),
        out_shape=[
            jax.ShapeDtypeStruct((local_dets, rows, COLS), f32),
            jax.ShapeDtypeStruct((local_dets, rows, COLS), f32),
            jax.ShapeDtypeStruct((tall, LOW), f32),
        ],
        in_specs=[smem, pl.BlockSpec(memory_space=pl.ANY), whole, whole],
        out_specs=[whole] * 3,
        scratch_shapes=[pltpu.VMEM((HALVES * rows * local_dets, LANES), f32)] * 2,
        compiler_params=vmem(32),
        cost_estimate=pl.CostEstimate(
            flops=2 * cells * tall * LOW * 8, bytes_accessed=16 * cells, transcendentals=0
        ),
        name="weights",
    )(inverse_white, fit_amps, tile_id, pixel_id)

    consts = [jnp.asarray(t) for t in tables(rows)]
    parts = len(received)
    fixed2 = lambda i, *_: (0, 0)
    by_det = lambda i, *_: (i, 0, 0)
    weighted_data, sky_part, weight_part = pl.pallas_call(
        functools.partial(filter_kernel, parts),
        out_shape=[
            jax.ShapeDtypeStruct((local_dets, full_length), bf16),
            jax.ShapeDtypeStruct((tile_count, PIX), f32),
            jax.ShapeDtypeStruct((tile_count, PIX), f32),
        ],
        grid_spec=pltpu.PrefetchScalarGridSpec(
            num_scalar_prefetch=4,
            grid=(local_dets,),
            in_specs=[pl.BlockSpec((1, *r.shape[1:]), by_det) for r in received]
            + [pl.BlockSpec((1, rows, COLS), by_det)] * 2
            + [pl.BlockSpec((tall, LOW), fixed2)]
            + [pl.BlockSpec(c.shape, fixed2) for c in consts],
            out_specs=[
                pl.BlockSpec((local_dets, full_length), fixed2),
                pl.BlockSpec((tile_count, PIX), fixed2),
                pl.BlockSpec((tile_count, PIX), fixed2),
            ],
            scratch_shapes=[
                pltpu.VMEM((rows, COLS), f32),
                pltpu.VMEM((HALVES * rows * local_dets, LANES), f32),
                pltpu.VMEM((tall, LOW), f32),
            ],
        ),
        compiler_params=vmem(48),
        name="filter_and_bin",
    )(place, tile_order, knee_freq, white_level, *received, high, low, weight_sum, *consts)

    owned = tile_count * PIX // owners
    both = jnp.concatenate(
        [sky_part.reshape(owners, owned), weight_part.reshape(owners, owned)], axis=1
    )
    spread = jnp.broadcast_to(both[None], (groups, *both.shape)).reshape(groups * owners, 2 * owned)
    spread = lax.all_to_all(spread, ("det", "tm"), split_axis=0, concat_axis=0, tiled=True)
    scale = float(tile_count * PIX) / float(local_dets * groups * owners * full_length)
    summed = jnp.sum(spread, axis=0) * scale
    return (fit_amps, weighted_data, summed[:owned], summed[owned:])


def solution(mesh):
    in_specs = (
        P("det", "tm"),
        P(None, None, "tm"),
        P("det"),
        P(("det", "tm")),
        P(("det", "tm")),
        P(("det", "tm"), None),
        P(("det", "tm"), None),
        P(),
    )
    out_specs = (P(None, "det"), P(("det", "tm"), None), P("tm"), P("tm"))
    return jax.shard_map(shards, mesh=mesh, in_specs=in_specs, out_specs=out_specs, check_vma=False)
```

```python
import functools
import math

import jax
import jax.numpy as jnp
import numpy as np
from jax import lax
from jax.experimental import pallas as pl
from jax.experimental.pallas import tpu as pltpu
from jax.sharding import PartitionSpec as P

PIX = 128
COLS = 256
LANES = 128
HALVES = COLS // LANES
LOW = 64
SAMPLE_RATE = 200.0
MIB = 1024 * 1024
NT = (((1,), (1,)), ((), ()))
f32 = jnp.float32
bf16 = jnp.bfloat16


def split2(x):
    high = x.astype(bf16)
    return high, (x - high.astype(f32)).astype(bf16)


def split3(x):
    high = x.astype(bf16)
    rest = x - high.astype(f32)
    mid = rest.astype(bf16)
    return high, mid, (rest - mid.astype(f32)).astype(bf16)


def host_split(x):
    high = x.astype(np.float32).astype(bf16)
    low = (x - high.astype(np.float64)).astype(np.float32).astype(bf16)
    return high, low


@functools.lru_cache(maxsize=None)
def tables(rows):
    total = rows * COLS
    half = rows // 2
    slots = np.arange(half)
    slots[0] = half
    ramp = np.arange(rows)
    angle = 2.0 * np.pi * (slots[:, None] * ramp[None, :] % rows) / rows
    first = np.concatenate([np.cos(angle), -np.sin(angle)], axis=0)
    first[half] = 1.0
    weight = np.full((half,), 2.0)
    weight[0] = 1.0
    last = np.concatenate([weight[:, None] * np.cos(angle), -2.0 * np.sin(angle)], axis=0)
    last[half] = 1.0
    last = last.T / total
    col = np.arange(COLS)
    phase = 2.0 * np.pi * (col[:, None] * col[None, :] % COLS) / COLS
    side = np.concatenate([np.cos(phase), np.sin(phase)], axis=1)
    turn = 2.0 * np.pi * (slots[:, None] * col[None, :] % total) / total
    bins = np.concatenate([slots, np.zeros((16,), np.int64)])[:, None] + rows * col[None, :]
    freq = np.minimum(bins, total - bins).astype(np.float32) * np.float32(SAMPLE_RATE / total)
    return (
        *host_split(first),
        *host_split(side),
        *host_split(last),
        np.cos(turn).astype(np.float32),
        np.sin(turn).astype(np.float32),
        (freq * freq).astype(np.float32),
    )


def dot3(left, right):
    (lh, ll), (rh, rl) = left, right
    return jnp.dot(
        jnp.concatenate([lh, ll, lh], axis=1),
        jnp.concatenate([rh, rh, rl], axis=0),
        preferred_element_type=f32,
    )


def pick(core, first, second):
    return jnp.where(core == 0, first, second)


def fit_kernel(runs, run_len, local_dets, paired, scalar_ref, data_ref, *refs):
    template_refs, out_ref = refs[:runs], refs[runs]
    parts, wide = [], []
    for run in range(runs):
        temp = template_refs[run][0]
        modes = temp.shape[0]
        high, mid, low = split3(data_ref[run * run_len : (run + 1) * run_len, :])
        both = lax.dot_general(
            temp, jnp.concatenate([temp, high, mid, low], axis=0), NT, preferred_element_type=f32
        )
        ends = [modes + i * run_len for i in range(4)]
        parts.append(both[:, :modes])
        parts.append(
            both[:, ends[0] : ends[1]] + both[:, ends[1] : ends[2]] + both[:, ends[2] : ends[3]]
        )
        wide.append(temp.astype(f32))
    part = jnp.concatenate(parts, axis=1)

    @pl.when(pl.program_id(0) == 0)
    def _():
        out_ref[...] = part

    @pl.when(pl.program_id(0) > 0)
    def _():
        out_ref[...] += part

    if paired:
        mine_ref, send_ref = refs[runs + 1 :]
        row_count = data_ref.shape[0]
        core = jnp.bitwise_and(scalar_ref[row_count], 1)
        groups = [
            data_ref[start : start + local_dets, :] for start in range(0, row_count, local_dets)
        ]
        even = jnp.concatenate(groups[0::2], axis=0)
        odd = jnp.concatenate(groups[1::2], axis=0)
        mine_ref[...] = pick(core, even, odd)
        send_ref[: row_count // 2, :] = pick(core, odd, even)
        send_ref[row_count // 2 :, :] = jnp.concatenate(wide, axis=0)


def eliminate(sums_ref, runs, run_len, modes):
    width = modes + run_len
    row_index = lax.broadcasted_iota(jnp.int32, (modes, width), 0)
    joined = [sums_ref[:, run * width : (run + 1) * width] for run in range(runs)]
    for column in range(modes):
        for run in range(runs):
            now = joined[run]
            pivot_row = now[column : column + 1, :] / now[column : column + 1, column : column + 1]
            rest = now - now[:, column : column + 1] * pivot_row
            joined[run] = jnp.where(row_index == column, pivot_row, rest)
    return [now[:, modes:] for now in joined]


def paired_kernel(runs, run_len, local_dets, chunks, scalar_ref, sums_ref, mine_ref, got_ref, *refs):
    template_refs, amps_ref = refs[:runs], refs[runs]
    out_refs, rows_ref = refs[runs + 1 : -1], refs[-1]
    modes = template_refs[0].shape[1]
    kept, time_local = mine_ref.shape
    pieces = time_local // COLS
    amps = eliminate(sums_ref, runs, run_len, modes)
    amps_ref[...] = jnp.concatenate(amps, axis=1)
    me = scalar_ref[2 * kept]
    core, chip = jnp.bitwise_and(me, 1), jnp.right_shift(me, 1)
    per_run = run_len // 2
    shard_rows = HALVES * pieces * kept
    for run in range(runs):
        turned = amps[run].T
        groups = [turned[start : start + local_dets] for start in range(0, run_len, local_dets)]
        turned = pick(
            core, jnp.concatenate(groups[0::2], axis=0), jnp.concatenate(groups[1::2], axis=0)
        )
        left = jnp.concatenate(split3(turned), axis=1)
        rows = slice(run * per_run, (run + 1) * per_run)
        other = got_ref[kept + run * modes : kept + (run + 1) * modes, :].astype(bf16)
        for side, (temp, data_ref) in enumerate([(template_refs[run][0], mine_ref), (other, got_ref)]):
            fitted = jnp.dot(left, jnp.concatenate([temp] * 3, axis=0), preferred_element_type=f32)
            for lane in range(time_local // LANES):
                cols = slice(lane * LANES, (lane + 1) * LANES)
                start = side * shard_rows + run * per_run
                start += (lane % HALVES * pieces + lane // HALVES) * kept
                rows_ref[start : start + per_run, :] = data_ref[rows, cols] - fitted[:, cols]
    chips = kept // local_dets
    per_chunk = local_dets // chunks
    for chunk in range(chunks):
        for step in range(chips):
            base = jnp.bitwise_xor(chip, step) * local_dets + chunk * per_chunk
            for det in range(per_chunk):
                for side in range(2):
                    place = pl.multiple_of(jnp.bitwise_xor(core, side) * pieces, pieces)
                    out_refs[chunk * chips + step][det, pl.ds(place, pieces), :] = take_rows(
                        rows_ref, side * shard_rows + base + det, pieces, kept
                    )


def residual_kernel(runs, run_len, owners, scalar_ref, sums_ref, data_ref, *refs):
    template_refs = refs[:runs]
    amps_ref, out_ref, rows_ref = refs[runs:]
    modes = template_refs[0].shape[1]
    row_count, time_local = data_ref.shape
    pieces = time_local // COLS
    amps = eliminate(sums_ref, runs, run_len, modes)
    amps_ref[...] = jnp.concatenate(amps, axis=1)
    for run in range(runs):
        temp = template_refs[run][0]
        left = jnp.concatenate(split3(amps[run].T), axis=1)
        fitted = jnp.dot(left, jnp.concatenate([temp] * 3, axis=0), preferred_element_type=f32)
        rows = slice(run * run_len, (run + 1) * run_len)
        for lane in range(time_local // LANES):
            cols = slice(lane * LANES, (lane + 1) * LANES)
            start = (lane % HALVES * pieces + lane // HALVES) * row_count + run * run_len
            rows_ref[start : start + run_len, :] = data_ref[rows, cols] - fitted[:, cols]
    local_dets = row_count // owners
    for owner in range(owners):
        for det in range(local_dets):
            out_ref[owner, det] = take_rows(rows_ref, owner * local_dets + det, pieces, row_count)


def take_rows(ref, start, count, stride):
    return jnp.concatenate(
        [
            ref[pl.ds(side * count * stride + start, count, stride=stride), :]
            for side in range(HALVES)
        ],
        axis=1,
    )


def binned(high_rows, low_rows, value_rows, weight_row, tall):
    high_ramp = lax.broadcasted_iota(jnp.int32, (tall, COLS), 0).astype(f32).astype(bf16)
    low_ramp = lax.broadcasted_iota(jnp.int32, (LOW, COLS), 0).astype(f32).astype(bf16)
    weight = jnp.broadcast_to(weight_row, (tall, COLS)).astype(bf16)
    zero, one = jnp.zeros((tall, COLS), bf16), jnp.ones((LOW, COLS), bf16)
    lefts, rights = [], []
    for row in range(high_rows.shape[0]):
        high = jnp.broadcast_to(high_rows[row : row + 1], (tall, COLS)).astype(bf16)
        low = jnp.broadcast_to(low_rows[row : row + 1], (LOW, COLS)).astype(bf16)
        value = jnp.broadcast_to(value_rows[row : row + 1], (tall, COLS)).astype(bf16)
        hot = high == high_ramp
        lefts.append(
            jnp.concatenate([jnp.where(hot, value, zero), jnp.where(hot, weight, zero)], axis=0)
        )
        rights.append(jnp.where(low == low_ramp, one, jnp.zeros_like(one)))
    return lax.dot_general(
        jnp.concatenate(lefts, axis=1),
        jnp.concatenate(rights, axis=1),
        NT,
        preferred_element_type=f32,
    )


def cell_kernel(after_ref, tile_ref, pixel_ref, high_ref, low_ref, hi_s, lo_s):
    local_dets, rows = high_ref.shape[0], high_ref.shape[1]
    cell = tile_ref[...] * PIX + pixel_ref[...]
    high = jnp.right_shift(cell, LOW.bit_length() - 1).astype(f32)
    low = jnp.bitwise_and(cell, LOW - 1).astype(f32)
    for lane in range(rows * HALVES):
        cols = slice(lane * LANES, (lane + 1) * LANES)
        start = (lane % HALVES * rows + lane // HALVES) * local_dets
        hi_s[start : start + local_dets, :] = high[:, cols]
        lo_s[start : start + local_dets, :] = low[:, cols]
    for det in range(local_dets):
        high_ref[det] = take_rows(hi_s, det, rows, local_dets)
        low_ref[det] = take_rows(lo_s, det, rows, local_dets)


def filter_kernel(parts, first_det, dets, final, place_ref, order_ref, knee_ref, white_ref, inverse_ref, *refs):
    part_refs = refs[:parts]
    (high_ref, low_ref, f_h, f_l, s_h, s_l, l_h, l_l, tc_ref, ts_ref, sq_ref) = refs[
        parts : parts + 11
    ]
    refs = refs[parts + 11 :]
    if first_det > 0:
        before_ref, sums_ref, refs = refs[0], refs[1], refs[2:]
    if final:
        out_ref, sky_ref, weight_ref, signal, stacked, totals = refs
    else:
        stacked, totals, signal = refs
    turn = pl.program_id(0)
    det = turn + first_det
    rows = signal.shape[0]
    half = rows // 2
    for part in range(parts):
        height = part_refs[part].shape[1]
        start = place_ref[part] * height if parts > 1 else 0
        if parts > 1:
            start = pl.multiple_of(start, height)
        signal[pl.ds(start, height), :] = part_refs[part][0]
    row_index = lax.broadcasted_iota(jnp.int32, (half, COLS), 0)
    turn_cos, turn_sin = tc_ref[...], ts_ref[...]
    side = (s_h[...], s_l[...])
    first = dot3((f_h[...], f_l[...]), split2(signal[...]))
    real_y, low_y = first[:half], first[half:]
    imag_y = jnp.where(row_index == 0, 0.0, low_y)
    zero_y = jnp.broadcast_to(low_y[0:1], (16, COLS))
    real_z = real_y * turn_cos + imag_y * turn_sin
    imag_z = imag_y * turn_cos - real_y * turn_sin
    forward = dot3(split2(jnp.concatenate([real_z, imag_z, zero_y], axis=0)), side)
    cos_f, sin_f = forward[:, :COLS], forward[:, COLS:]
    squared = sq_ref[...]
    knee = knee_ref[det]
    gain = squared / (white_ref[det] * (squared + knee * knee))
    gain_main, gain_zero = gain[:half], gain[half:]
    real_x = (cos_f[:half] + sin_f[half : 2 * half]) * gain_main
    imag_x = (cos_f[half : 2 * half] - sin_f[:half]) * gain_main
    zero_r = cos_f[2 * half :] * gain_zero
    zero_i = -sin_f[2 * half :] * gain_zero
    back = dot3(split2(jnp.concatenate([real_x, imag_x, zero_r, zero_i], axis=0)), side)
    cos_b, sin_b = back[:, :COLS], back[:, COLS:]
    real_u = cos_b[:half] - sin_b[half : 2 * half]
    imag_u = sin_b[:half] + cos_b[half : 2 * half]
    zero_o = cos_b[2 * half : 2 * half + 16] - sin_b[2 * half + 16 :]
    real_v = real_u * turn_cos - imag_u * turn_sin
    imag_v = real_u * turn_sin + imag_u * turn_cos
    imag_v = jnp.where(row_index == 0, zero_o[0:1], imag_v)
    result = dot3((l_h[...], l_l[...]), split2(jnp.concatenate([real_v, imag_v], axis=0)))
    signal[...] = result
    for half_index in range(HALVES):
        cols = slice(half_index * LANES, (half_index + 1) * LANES)
        stacked[pl.ds(half_index * rows * dets + det, rows, stride=dets), :] = result[:, cols]

    @pl.when(turn == 0)
    def _():
        totals[...] = sums_ref[...] if first_det > 0 else jnp.zeros_like(totals)

    tall = totals.shape[0] // 2
    weight_row = jnp.full((1, COLS), inverse_ref[det], f32)
    chunk = min(128, rows)

    @pl.loop(0, rows // chunk)
    def _(step):
        here = pl.ds(pl.multiple_of(step * chunk, chunk), chunk)
        totals[...] += binned(
            high_ref[0, here], low_ref[0, here], signal[here, :], weight_row, tall
        )

    if final:

        @pl.when(turn == pl.num_programs(0) - 1)
        def _():
            det_index = lax.broadcasted_iota(jnp.int32, (dets, LANES), 0)
            for lane in range(rows * HALVES):
                start = (lane % HALVES * rows + lane // HALVES) * dets
                here = stacked[start : start + dets, :]
                if first_det > 0:
                    here = jnp.where(
                        det_index < first_det, before_ref[start : start + dets, :], here
                    )
                out_ref[:, lane * LANES : (lane + 1) * LANES] = here.astype(bf16)
            per_tile = PIX // LOW
            for tile in range(sky_ref.shape[0]):
                source = order_ref[tile] * per_tile
                for piece in range(per_tile):
                    cols = slice(piece * LOW, (piece + 1) * LOW)
                    sky_ref[tile : tile + 1, cols] = totals[pl.ds(source + piece, 1), :]
                    weight_ref[tile : tile + 1, cols] = totals[pl.ds(tall + source + piece, 1), :]


def swap(x, step, axis):
    size = lax.axis_size(axis)
    return lax.ppermute(x, axis, [(i, i ^ step) for i in range(size)])


def vmem(limit):
    return pltpu.CompilerParams(vmem_limit_bytes=limit * MIB)


def shards(
    detector_data, templates, wafer_of, knee_freq, white_level, tile_id, pixel_id, tile_order
):
    row_count, time_local = detector_data.shape
    wafer_count, modes, _ = templates.shape
    owners, groups = lax.axis_size("tm"), lax.axis_size("det")
    run_len = min(row_count, row_count * groups // wafer_count)
    runs = row_count // run_len
    width = runs * (modes + run_len)
    local_dets = row_count // owners
    full_length = time_local * owners
    rows = full_length // COLS
    pieces = time_local // COLS
    me = lax.axis_index("tm").astype(jnp.int32)
    scalars = jnp.concatenate([wafer_of, me[None]])
    power = owners & (owners - 1) == 0
    paired = power and 4 <= owners <= 8 and run_len % (2 * local_dets) == 0
    step_len = min(2048, time_local)

    def template_spec(run, blocked):
        length = step_len if blocked else time_local
        return pl.BlockSpec(
            (1, modes, length),
            lambda i, w, run=run: (w[run * run_len], 0, i if blocked else 0),
        )

    def fixed(*shape):
        return pl.BlockSpec(shape, lambda i, *_: (0,) * len(shape))

    def by_step(height):
        return pl.BlockSpec((height, step_len), lambda i, w: (0, i))

    kept = row_count // 2
    sent = kept + runs * modes
    sums, *packed = pl.pallas_call(
        functools.partial(fit_kernel, runs, run_len, local_dets, paired),
        out_shape=[jax.ShapeDtypeStruct((modes, width), f32)]
        + [jax.ShapeDtypeStruct((n, time_local), f32) for n in (kept, sent) if paired],
        grid_spec=pltpu.PrefetchScalarGridSpec(
            num_scalar_prefetch=1,
            grid=(time_local // step_len,),
            in_specs=[by_step(row_count)] + [template_spec(run, True) for run in range(runs)],
            out_specs=[fixed(modes, width)] + [by_step(n) for n in (kept, sent) if paired],
        ),
        compiler_params=vmem(60),
        name="fit_sums",
    )(scalars, detector_data, *[templates] * runs)
    if paired:
        got = swap(packed[1], 1, "tm")
    if power:
        step = owners // 2
        while step > 0:
            sums = sums + swap(sums, step, "tm")
            step //= 2
    else:
        sums = lax.psum(sums, "tm")

    chunks = 2 if paired and local_dets % 2 == 0 else 1
    per_chunk = local_dets // chunks
    if paired:
        block_shape = (per_chunk, 2 * pieces, COLS)
        chips = owners // 2
        blocks_out = [block_shape] * (chunks * chips)
        kernel = functools.partial(paired_kernel, runs, run_len, local_dets, chunks)
        operands = [packed[0], got]
        operand_specs = [fixed(kept, time_local), fixed(sent, time_local)]
        scratch = pltpu.VMEM((2 * HALVES * pieces * kept, LANES), f32)
    else:
        blocks_out = [(owners, local_dets, pieces, COLS)]
        kernel = functools.partial(residual_kernel, runs, run_len, owners)
        operands = [detector_data]
        operand_specs = [fixed(row_count, time_local)]
        scratch = pltpu.VMEM((HALVES * pieces * row_count, LANES), f32)
    fit_amps, *blocks = pl.pallas_call(
        kernel,
        out_shape=[jax.ShapeDtypeStruct(shape, f32) for shape in [(modes, row_count), *blocks_out]],
        grid_spec=pltpu.PrefetchScalarGridSpec(
            num_scalar_prefetch=1,
            grid=(1,),
            in_specs=[fixed(modes, width), *operand_specs]
            + [template_spec(run, False) for run in range(runs)],
            out_specs=[fixed(modes, row_count)] + [fixed(*shape) for shape in blocks_out],
            scratch_shapes=[scratch],
        ),
        compiler_params=vmem(32),
        name="residual",
    )(scalars, sums, *operands, *[templates] * runs)

    if paired:
        received = []
        for chunk in range(chunks):
            here = blocks[chunk * chips : (chunk + 1) * chips]
            for step in reversed(range(1, chips)):
                here[step] = swap(here[step], 2 * step, "tm")
            received.append(here)
        place = jnp.bitwise_xor(me // 2, jnp.arange(chips, dtype=jnp.int32))
    else:
        moved = lax.all_to_all(blocks[0], "tm", split_axis=0, concat_axis=0, tiled=True)
        received = [[jnp.swapaxes(moved, 0, 1).reshape(local_dets, rows, COLS)]]
        place = jnp.zeros((1,), jnp.int32)

    tile_count = tile_order.shape[0]
    tall = tile_count * PIX // LOW
    inverse_white = (1.0 / white_level).astype(bf16).astype(f32)
    whole = pl.BlockSpec(memory_space=pltpu.VMEM)
    high, low = pl.pallas_call(
        cell_kernel,
        out_shape=[jax.ShapeDtypeStruct((local_dets, rows, COLS), f32)] * 2,
        in_specs=[pl.BlockSpec(memory_space=pl.ANY), whole, whole],
        out_specs=[whole] * 2,
        scratch_shapes=[pltpu.VMEM((HALVES * rows * local_dets, LANES), f32)] * 2,
        compiler_params=vmem(32),
        cost_estimate=pl.CostEstimate(
            flops=0, bytes_accessed=32 * local_dets * full_length, transcendentals=0
        ),
        name="cells",
    )(fit_amps, tile_id, pixel_id)

    consts = [jnp.asarray(t) for t in tables(rows)]
    stacked_shape = (HALVES * rows * local_dets, LANES)
    carried = []
    for chunk in range(chunks):
        final = chunk == chunks - 1
        first_det = chunk * per_chunk
        parts = len(received[chunk])
        if final:
            outs = [((local_dets, full_length), bf16)] + [((tile_count, PIX), f32)] * 2
            scratch = [pltpu.VMEM(s, f32) for s in ((rows, COLS), stacked_shape, (2 * tall, LOW))]
        else:
            outs = [(stacked_shape, f32), ((2 * tall, LOW), f32)]
            scratch = [pltpu.VMEM((rows, COLS), f32)]
        carried = pl.pallas_call(
            functools.partial(filter_kernel, parts, first_det, local_dets, final),
            out_shape=[jax.ShapeDtypeStruct(*o) for o in outs],
            grid_spec=pltpu.PrefetchScalarGridSpec(
                num_scalar_prefetch=5,
                grid=(per_chunk,),
                in_specs=[
                    pl.BlockSpec((1, *r.shape[1:]), lambda i, *_: (i, 0, 0))
                    for r in received[chunk]
                ]
                + [
                    pl.BlockSpec((1, rows, COLS), lambda i, *_, f=first_det: (i + f, 0, 0)),
                ]
                * 2
                + [fixed(*c.shape) for c in [*consts, *carried]],
                out_specs=[fixed(*shape) for shape, _ in outs],
                scratch_shapes=scratch,
            ),
            compiler_params=vmem(48),
            cost_estimate=pl.CostEstimate(
                flops=80000 * per_chunk * full_length,
                bytes_accessed=16 * per_chunk * full_length,
                transcendentals=0,
            ),
            name="filter_and_bin",
        )(
            place,
            tile_order,
            knee_freq,
            white_level,
            inverse_white,
            *received[chunk],
            high,
            low,
            *consts,
            *carried,
        )
    weighted_data, sky_part, weight_part = carried

    owned = tile_count * PIX // owners
    both = jnp.concatenate(
        [sky_part.reshape(owners, owned), weight_part.reshape(owners, owned)], axis=1
    )
    spread = jnp.broadcast_to(both[None], (groups, *both.shape)).reshape(groups * owners, 2 * owned)
    spread = lax.all_to_all(spread, ("det", "tm"), split_axis=0, concat_axis=0, tiled=True)
    scale = float(tile_count * PIX) / float(local_dets * groups * owners * full_length)
    summed = jnp.sum(spread, axis=0) * scale
    return (fit_amps, weighted_data, summed[:owned], summed[owned:])


def solution(mesh):
    in_specs = (
        P("det", "tm"),
        P(None, None, "tm"),
        P("det"),
        P(("det", "tm")),
        P(("det", "tm")),
        P(("det", "tm"), None),
        P(("det", "tm"), None),
        P(),
    )
    out_specs = (P(None, "det"), P(("det", "tm"), None), P("tm"), P("tm"))
    return jax.shard_map(shards, mesh=mesh, in_specs=in_specs, out_specs=out_specs, check_vma=False)
```

```python
import functools
import math

import jax
import jax.numpy as jnp
import numpy as np
from jax import lax
from jax.experimental import pallas as pl
from jax.experimental.pallas import tpu as pltpu
from jax.sharding import PartitionSpec as P

PIX = 128
COLS = 256
LANES = 128
HALVES = COLS // LANES
LOW = 64
SAMPLE_RATE = 200.0
MIB = 1024 * 1024
STEP = 8192
NT = (((1,), (1,)), ((), ()))
f32 = jnp.float32
bf16 = jnp.bfloat16


def split2(x):
    high = x.astype(bf16)
    return high, (x - high.astype(f32)).astype(bf16)


def split3(x):
    high = x.astype(bf16)
    rest = x - high.astype(f32)
    mid = rest.astype(bf16)
    return high, mid, (rest - mid.astype(f32)).astype(bf16)


@functools.lru_cache(maxsize=None)
def tables(rows):
    total = rows * COLS
    half = rows // 2
    slots = np.arange(half)
    slots[0] = half
    ramp = np.arange(rows)
    angle = 2.0 * np.pi * (slots[:, None] * ramp[None, :] % rows) / rows
    first = np.concatenate([np.cos(angle), -np.sin(angle)], axis=0)
    first[half] = 1.0
    weight = np.full((half,), 2.0)
    weight[0] = 1.0
    last = np.concatenate([weight[:, None] * np.cos(angle), -2.0 * np.sin(angle)], axis=0)
    last[half] = 1.0
    last = last.T / total
    col = np.arange(COLS)
    phase = 2.0 * np.pi * (col[:, None] * col[None, :] % COLS) / COLS
    turn = 2.0 * np.pi * (slots[:, None] * col[None, :] % total) / total
    bins = np.concatenate([slots, np.zeros((16,), np.int64)])[:, None] + rows * col[None, :]
    freq = np.minimum(bins, total - bins).astype(np.float32) * np.float32(SAMPLE_RATE / total)
    made = [first, np.cos(phase), np.sin(phase), last, np.cos(turn), np.sin(turn), freq * freq]
    return np.concatenate([table.astype(np.float32) for table in made], axis=0)


def dot3(left, right):
    (lh, ll), (rh, rl) = left, right
    return jnp.dot(
        jnp.concatenate([lh, ll, lh], axis=1),
        jnp.concatenate([rh, rh, rl], axis=0),
        preferred_element_type=f32,
    )


def fit_kernel(runs, run_len, paired, wafer_ref, data_ref, *refs):
    template_refs, out_ref = refs[:runs], refs[runs]
    parts = []
    for run in range(runs):
        temp = template_refs[run][0]
        modes = temp.shape[0]
        high, mid, low = split3(data_ref[run * run_len : (run + 1) * run_len, :])
        both = lax.dot_general(
            temp, jnp.concatenate([temp, high, mid, low], axis=0), NT, preferred_element_type=f32
        )
        ends = [modes + i * run_len for i in range(4)]
        parts.append(both[:, :modes])
        parts.append(
            both[:, ends[0] : ends[1]] + both[:, ends[1] : ends[2]] + both[:, ends[2] : ends[3]]
        )
        if paired:
            refs[runs + 1][run * modes : (run + 1) * modes, :] = temp.astype(f32)
    part = jnp.concatenate(parts, axis=1)

    @pl.when(pl.program_id(0) == 0)
    def _():
        out_ref[...] = part

    @pl.when(pl.program_id(0) > 0)
    def _():
        out_ref[...] += part


def eliminate(sums, runs, run_len, modes):
    width = modes + run_len
    row_index = lax.broadcasted_iota(jnp.int32, (modes, width), 0)
    joined = [sums[:, run * width : (run + 1) * width] for run in range(runs)]
    for column in range(modes):
        for run in range(runs):
            now = joined[run]
            pivot_row = now[column : column + 1, :] / now[column : column + 1, column : column + 1]
            rest = now - now[:, column : column + 1] * pivot_row
            joined[run] = jnp.where(row_index == column, pivot_row, rest)
    return [now[:, modes:] for now in joined]


def paired_kernel(
    runs, run_len, local_dets, chunks, wafer_ref, data_ref, got_ref, wide_ref, temp_ref, *refs
):
    chips = data_ref.shape[0] // (2 * local_dets)
    terms, refs = [ref[...] for ref in refs[:chips]], refs[chips:]
    while len(terms) > 1:
        terms = [a + b for a, b in zip(terms[0::2], terms[1::2])]
    amps_ref, out_refs, rows_ref = refs[0], refs[1:-1], refs[-1]
    modes = temp_ref.shape[1]
    row_count, time_local = data_ref.shape
    kept = row_count // 2
    pieces = time_local // COLS
    amps = eliminate(terms[0], runs, run_len, modes)
    amps_ref[...] = jnp.concatenate(amps, axis=1)
    me = lax.axis_index("tm")
    core, chip = jnp.bitwise_and(me, 1), jnp.right_shift(me, 1)
    per_run = run_len // 2
    shard_rows = HALVES * pieces * kept

    def mine(rows):
        groups = [rows[start : start + local_dets] for start in range(0, run_len, local_dets)]
        even, odd = jnp.concatenate(groups[0::2], axis=0), jnp.concatenate(groups[1::2], axis=0)
        return jnp.where(core == 0, even, odd)

    for run in range(runs):
        left = jnp.concatenate(split3(mine(amps[run].T)), axis=1)
        own = temp_ref[wafer_ref[run * run_len]]
        other = wide_ref[run * modes : (run + 1) * modes, :].astype(bf16)
        for side, (temp, source) in enumerate([(own, data_ref), (other, got_ref)]):
            fitted = jnp.dot(left, jnp.concatenate([temp] * 3, axis=0), preferred_element_type=f32)
            kept_rows = mine(source[run * run_len : (run + 1) * run_len, :]) - fitted
            for lane in range(time_local // LANES):
                start = side * shard_rows + run * per_run
                start += (lane % HALVES * pieces + lane // HALVES) * kept
                rows_ref[start : start + per_run, :] = kept_rows[:, lane * LANES : (lane + 1) * LANES]
    per_chunk = local_dets // chunks
    for chunk in range(chunks):
        for step in range(chips):
            base = jnp.bitwise_xor(chip, step) * local_dets + chunk * per_chunk
            for det in range(per_chunk):
                for side in range(2):
                    place = pl.multiple_of(jnp.bitwise_xor(core, side) * pieces, pieces)
                    out_refs[chunk * chips + step][det, pl.ds(place, pieces), :] = take_rows(
                        rows_ref, side * shard_rows + base + det, pieces, kept
                    )


def residual_kernel(runs, run_len, owners, wafer_ref, data_ref, temp_ref, sums_ref, *refs):
    amps_ref, out_ref, rows_ref = refs
    modes = temp_ref.shape[1]
    row_count, time_local = data_ref.shape
    pieces = time_local // COLS
    amps = eliminate(sums_ref[...], runs, run_len, modes)
    amps_ref[...] = jnp.concatenate(amps, axis=1)
    for run in range(runs):
        temp = temp_ref[wafer_ref[run * run_len]]
        left = jnp.concatenate(split3(amps[run].T), axis=1)
        fitted = jnp.dot(left, jnp.concatenate([temp] * 3, axis=0), preferred_element_type=f32)
        rows = slice(run * run_len, (run + 1) * run_len)
        for lane in range(time_local // LANES):
            cols = slice(lane * LANES, (lane + 1) * LANES)
            start = (lane % HALVES * pieces + lane // HALVES) * row_count + run * run_len
            rows_ref[start : start + run_len, :] = data_ref[rows, cols] - fitted[:, cols]
    local_dets = row_count // owners
    for owner in range(owners):
        for det in range(local_dets):
            out_ref[owner, det] = take_rows(rows_ref, owner * local_dets + det, pieces, row_count)


def take_rows(ref, start, count, stride):
    return jnp.concatenate(
        [
            ref[pl.ds(side * count * stride + start, count, stride=stride), :]
            for side in range(HALVES)
        ],
        axis=1,
    )


def binned(high_rows, low_rows, value_rows, weight_row, tall):
    high_ramp = lax.broadcasted_iota(jnp.int32, (tall, COLS), 0).astype(f32).astype(bf16)
    low_ramp = lax.broadcasted_iota(jnp.int32, (LOW, COLS), 0).astype(f32).astype(bf16)
    weight = jnp.broadcast_to(weight_row, (tall, COLS)).astype(bf16)
    zero, one = jnp.zeros((tall, COLS), bf16), jnp.ones((LOW, COLS), bf16)
    lefts, rights = [], []
    for row in range(high_rows.shape[0]):
        high = jnp.broadcast_to(high_rows[row : row + 1], (tall, COLS)).astype(bf16)
        low = jnp.broadcast_to(low_rows[row : row + 1], (LOW, COLS)).astype(bf16)
        value = jnp.broadcast_to(value_rows[row : row + 1], (tall, COLS)).astype(bf16)
        hot = high == high_ramp
        lefts.append(
            jnp.concatenate([jnp.where(hot, value, zero), jnp.where(hot, weight, zero)], axis=0)
        )
        rights.append(jnp.where(low == low_ramp, one, jnp.zeros_like(one)))
    return lax.dot_general(
        jnp.concatenate(lefts, axis=1),
        jnp.concatenate(rights, axis=1),
        NT,
        preferred_element_type=f32,
    )


def prepare_kernel(knee_ref, white_ref, after_ref, table_ref, tile_ref, pixel_ref, *refs):
    outs, (turn_cos, turn_sin, gain_ref, inverse_ref, high_ref, low_ref, hi_s, lo_s) = refs[:6], refs[6:]
    local_dets, rows = high_ref.shape[0], high_ref.shape[1]
    half = rows // 2
    tables_at = [0]
    for height in (rows, COLS, COLS, rows, half, half):
        tables_at.append(tables_at[-1] + height)
    first, cosine, sine, last, turn_c, turn_s = (
        table_ref[start:end, :] for start, end in zip(tables_at[:-1], tables_at[1:])
    )
    for i, table in enumerate((first, jnp.concatenate([cosine, sine], axis=1), last)):
        outs[2 * i][...], outs[2 * i + 1][...] = split2(table)
    turn_cos[...], turn_sin[...] = turn_c, turn_s
    squared = table_ref[tables_at[-1] :, :]
    cell = tile_ref[...] * PIX + pixel_ref[...]
    high = jnp.right_shift(cell, LOW.bit_length() - 1).astype(f32)
    low = jnp.bitwise_and(cell, LOW - 1).astype(f32)
    for lane in range(rows * HALVES):
        cols = slice(lane * LANES, (lane + 1) * LANES)
        start = (lane % HALVES * rows + lane // HALVES) * local_dets
        hi_s[start : start + local_dets, :] = high[:, cols]
        lo_s[start : start + local_dets, :] = low[:, cols]
    for det in range(local_dets):
        high_ref[det] = take_rows(hi_s, det, rows, local_dets)
        low_ref[det] = take_rows(lo_s, det, rows, local_dets)
        knee = knee_ref[det]
        gain_ref[det] = squared / (white_ref[det] * (squared + knee * knee))
        inverse_ref[det] = 1.0 / jnp.full((1, COLS), white_ref[det], f32)


def filter_kernel(parts, first_det, count, dets, final, order_ref, *refs):
    part_refs = refs[:parts]
    (f_h, f_l, s_h, s_l, l_h, l_l, tc_ref, ts_ref, gain_ref, inverse_ref, high_ref, low_ref) = refs[
        parts : parts + 12
    ]
    refs = refs[parts + 12 :]
    if first_det > 0:
        before_ref, sums_ref, refs = refs[0], refs[1], refs[2:]
    if final:
        out_ref, sky_ref, weight_ref, signal, stacked, totals = refs
    else:
        stacked, totals, signal = refs
    rows = signal.shape[0]
    half = rows // 2
    totals[...] = sums_ref[...] if first_det > 0 else jnp.zeros_like(totals)
    tall = totals.shape[0] // 2
    row_index = lax.broadcasted_iota(jnp.int32, (half, COLS), 0)
    chip = jnp.right_shift(lax.axis_index("tm"), 1)

    def one(turn):
        det = turn + first_det
        for part in range(parts):
            height = part_refs[part].shape[1]
            start = 0
            if parts > 1:
                start = pl.multiple_of(jnp.bitwise_xor(chip, part) * height, height)
            signal[pl.ds(start, height), :] = part_refs[part][turn]
        turn_cos, turn_sin = tc_ref[...], ts_ref[...]
        side = (s_h[...], s_l[...])
        first = dot3((f_h[...], f_l[...]), split2(signal[...]))
        real_y, low_y = first[:half], first[half:]
        imag_y = jnp.where(row_index == 0, 0.0, low_y)
        zero_y = jnp.broadcast_to(low_y[0:1], (16, COLS))
        real_z = real_y * turn_cos + imag_y * turn_sin
        imag_z = imag_y * turn_cos - real_y * turn_sin
        forward = dot3(split2(jnp.concatenate([real_z, imag_z, zero_y], axis=0)), side)
        cos_f, sin_f = forward[:, :COLS], forward[:, COLS:]
        gain = gain_ref[det]
        gain_main, gain_zero = gain[:half], gain[half:]
        real_x = (cos_f[:half] + sin_f[half : 2 * half]) * gain_main
        imag_x = (cos_f[half : 2 * half] - sin_f[:half]) * gain_main
        zero_r = cos_f[2 * half :] * gain_zero
        zero_i = -sin_f[2 * half :] * gain_zero
        back = dot3(split2(jnp.concatenate([real_x, imag_x, zero_r, zero_i], axis=0)), side)
        cos_b, sin_b = back[:, :COLS], back[:, COLS:]
        real_u = cos_b[:half] - sin_b[half : 2 * half]
        imag_u = sin_b[:half] + cos_b[half : 2 * half]
        zero_o = cos_b[2 * half : 2 * half + 16] - sin_b[2 * half + 16 :]
        real_v = real_u * turn_cos - imag_u * turn_sin
        imag_v = real_u * turn_sin + imag_u * turn_cos
        imag_v = jnp.where(row_index == 0, zero_o[0:1], imag_v)
        result = dot3((l_h[...], l_l[...]), split2(jnp.concatenate([real_v, imag_v], axis=0)))
        signal[...] = result
        for half_index in range(HALVES):
            cols = slice(half_index * LANES, (half_index + 1) * LANES)
            stacked[pl.ds(half_index * rows * dets + det, rows, stride=dets), :] = result[:, cols]
        totals[...] += binned(high_ref[det], low_ref[det], result, inverse_ref[det], tall)

    for turn in range(count):
        one(turn)
    if final:
        det_index = lax.broadcasted_iota(jnp.int32, (dets, LANES), 0)
        for lane in range(rows * HALVES):
            start = (lane % HALVES * rows + lane // HALVES) * dets
            here = stacked[start : start + dets, :]
            if first_det > 0:
                here = jnp.where(det_index < first_det, before_ref[start : start + dets, :], here)
            out_ref[:, lane * LANES : (lane + 1) * LANES] = here.astype(bf16)
        per_tile = PIX // LOW
        for tile in range(sky_ref.shape[0]):
            source = order_ref[tile] * per_tile
            for piece in range(per_tile):
                cols = slice(piece * LOW, (piece + 1) * LOW)
                sky_ref[tile : tile + 1, cols] = totals[pl.ds(source + piece, 1), :]
                weight_ref[tile : tile + 1, cols] = totals[pl.ds(tall + source + piece, 1), :]


def swap(x, step, axis):
    size = lax.axis_size(axis)
    return lax.ppermute(x, axis, [(i, i ^ step) for i in range(size)])


def vmem(limit):
    return pltpu.CompilerParams(vmem_limit_bytes=limit * MIB)


def shards(
    detector_data, templates, wafer_of, knee_freq, white_level, tile_id, pixel_id, tile_order
):
    row_count, time_local = detector_data.shape
    wafer_count, modes, _ = templates.shape
    owners, groups = lax.axis_size("tm"), lax.axis_size("det")
    run_len = min(row_count, row_count * groups // wafer_count)
    runs = row_count // run_len
    width = runs * (modes + run_len)
    local_dets = row_count // owners
    full_length = time_local * owners
    rows = full_length // COLS
    pieces = time_local // COLS
    paired = owners & (owners - 1) == 0 and 4 <= owners <= 8 and run_len % (2 * local_dets) == 0
    step_len = min(STEP, time_local)
    smem = pl.BlockSpec(memory_space=pltpu.SMEM)
    whole = pl.BlockSpec(memory_space=pltpu.VMEM)
    anywhere = pl.BlockSpec(memory_space=pl.ANY)

    def template_spec(run):
        return pl.BlockSpec((1, modes, step_len), lambda i, w, run=run: (w[run * run_len], 0, i))

    def by_step(height):
        return pl.BlockSpec((height, step_len), lambda i, w: (0, i))

    if paired:
        got = swap(detector_data, 1, "tm")
    sums, *wide = pl.pallas_call(
        functools.partial(fit_kernel, runs, run_len, paired),
        out_shape=[jax.ShapeDtypeStruct((modes, width), f32)]
        + [jax.ShapeDtypeStruct((runs * modes, time_local), f32)] * paired,
        grid_spec=pltpu.PrefetchScalarGridSpec(
            num_scalar_prefetch=1,
            grid=(time_local // step_len,),
            in_specs=[by_step(row_count)] + [template_spec(run) for run in range(runs)],
            out_specs=[pl.BlockSpec((modes, width), lambda i, w: (0, 0))]
            + [by_step(runs * modes)] * paired,
        ),
        compiler_params=vmem(60),
        name="fit_sums",
    )(wafer_of, detector_data, *[templates] * runs)
    if paired:
        wide = swap(wide[0], 1, "tm")
    if paired:
        sums = sums + swap(sums, 1, "tm")
        sums = [sums] + [swap(sums, step, "tm") for step in range(2, owners, 2)]
    else:
        sums = [lax.psum(sums, "tm")]

    chunks = 2 if paired and local_dets % 2 == 0 else 1
    per_chunk = local_dets // chunks
    if paired:
        chips = owners // 2
        blocks_out = [(per_chunk, 2 * pieces, COLS)] * (chunks * chips)
        kernel = functools.partial(paired_kernel, runs, run_len, local_dets, chunks)
        operands = [detector_data, got, wide, templates]
        scratch = pltpu.VMEM((HALVES * pieces * row_count, LANES), f32)
    else:
        blocks_out = [(owners, local_dets, pieces, COLS)]
        kernel = functools.partial(residual_kernel, runs, run_len, owners)
        operands = [detector_data, templates]
        scratch = pltpu.VMEM((HALVES * pieces * row_count, LANES), f32)
    fit_amps, *blocks = pl.pallas_call(
        kernel,
        out_shape=[jax.ShapeDtypeStruct(shape, f32) for shape in [(modes, row_count), *blocks_out]],
        in_specs=[smem] + [whole] * (len(sums) + len(operands)),
        out_specs=[whole] * (1 + len(blocks_out)),
        scratch_shapes=[scratch],
        compiler_params=vmem(32),
        name="residual",
    )(wafer_of, *operands, *sums)

    if paired:
        received = [blocks[chunk * chips : (chunk + 1) * chips] for chunk in range(chunks)]
        for step in reversed(range(1, chips)):
            received[0][step] = swap(received[0][step], 2 * step, "tm")
    else:
        moved = lax.all_to_all(blocks[0], "tm", split_axis=0, concat_axis=0, tiled=True)
        received = [[jnp.swapaxes(moved, 0, 1).reshape(local_dets, rows, COLS)]]

    tile_count = tile_order.shape[0]
    tall = tile_count * PIX // LOW
    table = jnp.asarray(tables(rows))
    half = rows // 2
    grid_shape = (local_dets, rows, COLS)
    pair_shapes = [(rows, rows), (COLS, 2 * COLS), (rows, rows)]
    pairs = [jax.ShapeDtypeStruct(shape, bf16) for shape in pair_shapes for _ in range(2)]
    prepared_shapes = [
        (half, COLS),
        (half, COLS),
        (local_dets, half + 16, COLS),
        (local_dets, 1, COLS),
        grid_shape,
        grid_shape,
    ]
    prepared = pl.pallas_call(
        prepare_kernel,
        out_shape=pairs + [jax.ShapeDtypeStruct(shape, f32) for shape in prepared_shapes],
        in_specs=[smem, smem, anywhere, whole, whole, whole],
        out_specs=[whole] * 12,
        scratch_shapes=[pltpu.VMEM((HALVES * rows * local_dets, LANES), f32)] * 2,
        compiler_params=vmem(32),
        cost_estimate=pl.CostEstimate(
            flops=0, bytes_accessed=32 * local_dets * full_length, transcendentals=0
        ),
        name="prepare",
    )(knee_freq, white_level, fit_amps, table, tile_id, pixel_id)

    for chunk in range(1, chunks):
        received, prepared = lax.optimization_barrier((received, prepared))
        for step in reversed(range(1, chips)):
            received[chunk][step] = swap(received[chunk][step], 2 * step, "tm")

    stacked_shape = (HALVES * rows * local_dets, LANES)
    carried = []
    for chunk in range(chunks):
        final = chunk == chunks - 1
        first_det = chunk * per_chunk
        parts = len(received[chunk])
        if final:
            outs = [((local_dets, full_length), bf16)] + [((tile_count, PIX), f32)] * 2
            scratch = [pltpu.VMEM(s, f32) for s in ((rows, COLS), stacked_shape, (2 * tall, LOW))]
        else:
            outs = [(stacked_shape, f32), ((2 * tall, LOW), f32)]
            scratch = [pltpu.VMEM((rows, COLS), f32)]
        operands = [*received[chunk], *prepared, *carried]
        carried = pl.pallas_call(
            functools.partial(filter_kernel, parts, first_det, per_chunk, local_dets, final),
            out_shape=[jax.ShapeDtypeStruct(*o) for o in outs],
            in_specs=[smem] + [whole] * len(operands),
            out_specs=[whole] * len(outs),
            scratch_shapes=scratch,
            compiler_params=vmem(32),
            cost_estimate=pl.CostEstimate(
                flops=80000 * per_chunk * full_length,
                bytes_accessed=16 * per_chunk * full_length,
                transcendentals=0,
            ),
            name="filter_and_bin",
        )(tile_order, *operands)
    weighted_data, sky_part, weight_part = carried

    owned = tile_count * PIX // owners
    both = jnp.concatenate(
        [sky_part.reshape(owners, owned), weight_part.reshape(owners, owned)], axis=1
    )
    spread = jnp.broadcast_to(both[None], (groups, *both.shape)).reshape(groups * owners, 2 * owned)
    spread = lax.all_to_all(spread, ("det", "tm"), split_axis=0, concat_axis=0, tiled=True)
    scale = float(tile_count * PIX) / float(local_dets * groups * owners * full_length)
    summed = jnp.sum(spread, axis=0) * scale
    return (fit_amps, weighted_data, summed[:owned], summed[owned:])


def solution(mesh):
    in_specs = (
        P("det", "tm"),
        P(None, None, "tm"),
        P("det"),
        P(("det", "tm")),
        P(("det", "tm")),
        P(("det", "tm"), None),
        P(("det", "tm"), None),
        P(),
    )
    out_specs = (P(None, "det"), P(("det", "tm"), None), P("tm"), P("tm"))
    return jax.shard_map(shards, mesh=mesh, in_specs=in_specs, out_specs=out_specs, check_vma=False)
```

```python
import functools
import math

import jax
import jax.numpy as jnp
import numpy as np
from jax import lax
from jax.experimental import pallas as pl
from jax.experimental.pallas import tpu as pltpu
from jax.sharding import PartitionSpec as P

PIX = 128
COLS = 256
LANES = 128
HALVES = COLS // LANES
LOW = 64
SAMPLE_RATE = 200.0
MIB = 1024 * 1024
STEP = 8192
NT = (((1,), (1,)), ((), ()))
f32 = jnp.float32
bf16 = jnp.bfloat16


def split2(x):
    high = x.astype(bf16)
    return high, (x - high.astype(f32)).astype(bf16)


def split3(x):
    high = x.astype(bf16)
    rest = x - high.astype(f32)
    mid = rest.astype(bf16)
    return high, mid, (rest - mid.astype(f32)).astype(bf16)


@functools.lru_cache(maxsize=None)
def tables(rows):
    total = rows * COLS
    half = rows // 2
    slots = np.arange(half)
    slots[0] = half
    ramp = np.arange(rows)
    angle = 2.0 * np.pi * (slots[:, None] * ramp[None, :] % rows) / rows
    first = np.concatenate([np.cos(angle), -np.sin(angle)], axis=0)
    first[half] = 1.0
    weight = np.full((half,), 2.0)
    weight[0] = 1.0
    last = np.concatenate([weight[:, None] * np.cos(angle), -2.0 * np.sin(angle)], axis=0)
    last[half] = 1.0
    last = last.T / total
    col = np.arange(COLS)
    phase = 2.0 * np.pi * (col[:, None] * col[None, :] % COLS) / COLS
    turn = 2.0 * np.pi * (slots[:, None] * col[None, :] % total) / total
    bins = np.concatenate([slots, np.zeros((16,), np.int64)])[:, None] + rows * col[None, :]
    freq = np.minimum(bins, total - bins).astype(np.float32) * np.float32(SAMPLE_RATE / total)
    made = [first, np.cos(phase), np.sin(phase), last, np.cos(turn), np.sin(turn), freq * freq]
    return np.concatenate([table.astype(np.float32) for table in made], axis=0)


def dot3(left, right):
    (lh, ll), (rh, rl) = left, right
    return jnp.dot(
        jnp.concatenate([lh, ll, lh], axis=1),
        jnp.concatenate([rh, rh, rl], axis=0),
        preferred_element_type=f32,
    )


def fit_kernel(runs, run_len, paired, wafer_ref, data_ref, *refs):
    template_refs, out_ref = refs[:runs], refs[runs]
    parts = []
    for run in range(runs):
        temp = template_refs[run][0]
        modes = temp.shape[0]
        high, mid, low = split3(data_ref[run * run_len : (run + 1) * run_len, :])
        both = lax.dot_general(
            temp, jnp.concatenate([temp, high, mid, low], axis=0), NT, preferred_element_type=f32
        )
        ends = [modes + i * run_len for i in range(4)]
        parts.append(both[:, :modes])
        parts.append(
            both[:, ends[0] : ends[1]] + both[:, ends[1] : ends[2]] + both[:, ends[2] : ends[3]]
        )
        if paired:
            refs[runs + 1][run * modes : (run + 1) * modes, :] = temp.astype(f32)
    part = jnp.concatenate(parts, axis=1)

    @pl.when(pl.program_id(0) == 0)
    def _():
        out_ref[...] = part

    @pl.when(pl.program_id(0) > 0)
    def _():
        out_ref[...] += part


def eliminate(sums, runs, run_len, modes):
    width = modes + run_len
    row_index = lax.broadcasted_iota(jnp.int32, (modes, width), 0)
    joined = [sums[:, run * width : (run + 1) * width] for run in range(runs)]
    for column in range(modes):
        for run in range(runs):
            now = joined[run]
            pivot_row = now[column : column + 1, :] / now[column : column + 1, column : column + 1]
            rest = now - now[:, column : column + 1] * pivot_row
            joined[run] = jnp.where(row_index == column, pivot_row, rest)
    return [now[:, modes:] for now in joined]


def paired_kernel(
    runs, run_len, local_dets, chunks, wafer_ref, data_ref, got_ref, wide_ref, temp_ref, *refs
):
    chips = data_ref.shape[0] // (2 * local_dets)
    sums, refs = refs[0][...] + refs[1][...], refs[2:]
    amps_ref, out_refs, rows_ref = refs[0], refs[1:-1], refs[-1]
    modes = temp_ref.shape[1]
    row_count, time_local = data_ref.shape
    kept = row_count // 2
    pieces = time_local // COLS
    amps = eliminate(sums, runs, run_len, modes)
    amps_ref[...] = jnp.concatenate(amps, axis=1)
    me = lax.axis_index("tm")
    core, chip = jnp.bitwise_and(me, 1), jnp.right_shift(me, 1)
    per_run = run_len // 2
    shard_rows = HALVES * pieces * kept

    def mine(rows):
        groups = [rows[start : start + local_dets] for start in range(0, run_len, local_dets)]
        even, odd = jnp.concatenate(groups[0::2], axis=0), jnp.concatenate(groups[1::2], axis=0)
        return jnp.where(core == 0, even, odd)

    for run in range(runs):
        left = jnp.concatenate(split3(mine(amps[run].T)), axis=1)
        own = temp_ref[wafer_ref[run * run_len]]
        other = wide_ref[run * modes : (run + 1) * modes, :].astype(bf16)
        for side, (temp, source) in enumerate([(own, data_ref), (other, got_ref)]):
            fitted = jnp.dot(left, jnp.concatenate([temp] * 3, axis=0), preferred_element_type=f32)
            kept_rows = mine(source[run * run_len : (run + 1) * run_len, :]) - fitted
            for lane in range(time_local // LANES):
                start = side * shard_rows + run * per_run
                start += (lane % HALVES * pieces + lane // HALVES) * kept
                rows_ref[start : start + per_run, :] = kept_rows[:, lane * LANES : (lane + 1) * LANES]
    per_chunk = local_dets // chunks
    for chunk in range(chunks):
        for step in range(chips):
            base = jnp.bitwise_xor(chip, step) * local_dets + chunk * per_chunk
            for det in range(per_chunk):
                for side in range(2):
                    place = pl.multiple_of(jnp.bitwise_xor(core, side) * pieces, pieces)
                    out_refs[chunk * chips + step][det, pl.ds(place, pieces), :] = take_rows(
                        rows_ref, side * shard_rows + base + det, pieces, kept
                    )


def residual_kernel(runs, run_len, owners, wafer_ref, data_ref, temp_ref, sums_ref, *refs):
    amps_ref, out_ref, rows_ref = refs
    modes = temp_ref.shape[1]
    row_count, time_local = data_ref.shape
    pieces = time_local // COLS
    amps = eliminate(sums_ref[...], runs, run_len, modes)
    amps_ref[...] = jnp.concatenate(amps, axis=1)
    for run in range(runs):
        temp = temp_ref[wafer_ref[run * run_len]]
        left = jnp.concatenate(split3(amps[run].T), axis=1)
        fitted = jnp.dot(left, jnp.concatenate([temp] * 3, axis=0), preferred_element_type=f32)
        rows = slice(run * run_len, (run + 1) * run_len)
        for lane in range(time_local // LANES):
            cols = slice(lane * LANES, (lane + 1) * LANES)
            start = (lane % HALVES * pieces + lane // HALVES) * row_count + run * run_len
            rows_ref[start : start + run_len, :] = data_ref[rows, cols] - fitted[:, cols]
    local_dets = row_count // owners
    for owner in range(owners):
        for det in range(local_dets):
            out_ref[owner, det] = take_rows(rows_ref, owner * local_dets + det, pieces, row_count)


def take_rows(ref, start, count, stride):
    return jnp.concatenate(
        [
            ref[pl.ds(side * count * stride + start, count, stride=stride), :]
            for side in range(HALVES)
        ],
        axis=1,
    )


def binned(high_rows, low_rows, value_rows, weight_row, tall):
    high_ramp = lax.broadcasted_iota(jnp.int32, (tall, COLS), 0).astype(f32).astype(bf16)
    low_ramp = lax.broadcasted_iota(jnp.int32, (LOW, COLS), 0).astype(f32).astype(bf16)
    weight = jnp.broadcast_to(weight_row, (tall, COLS)).astype(bf16)
    zero, one = jnp.zeros((tall, COLS), bf16), jnp.ones((LOW, COLS), bf16)
    lefts, rights = [], []
    for row in range(high_rows.shape[0]):
        high = jnp.broadcast_to(high_rows[row : row + 1], (tall, COLS)).astype(bf16)
        low = jnp.broadcast_to(low_rows[row : row + 1], (LOW, COLS)).astype(bf16)
        value = jnp.broadcast_to(value_rows[row : row + 1], (tall, COLS)).astype(bf16)
        hot = high == high_ramp
        lefts.append(
            jnp.concatenate([jnp.where(hot, value, zero), jnp.where(hot, weight, zero)], axis=0)
        )
        rights.append(jnp.where(low == low_ramp, one, jnp.zeros_like(one)))
    return lax.dot_general(
        jnp.concatenate(lefts, axis=1),
        jnp.concatenate(rights, axis=1),
        NT,
        preferred_element_type=f32,
    )


def prepare_kernel(knee_ref, white_ref, after_ref, table_ref, tile_ref, pixel_ref, *refs):
    outs, (turn_cos, turn_sin, gain_ref, inverse_ref, high_ref, low_ref, hi_s, lo_s) = refs[:6], refs[6:]
    local_dets, rows = high_ref.shape[0], high_ref.shape[1]
    half = rows // 2
    tables_at = [0]
    for height in (rows, COLS, COLS, rows, half, half):
        tables_at.append(tables_at[-1] + height)
    first, cosine, sine, last, turn_c, turn_s = (
        table_ref[start:end, :] for start, end in zip(tables_at[:-1], tables_at[1:])
    )
    for i, table in enumerate((first, jnp.concatenate([cosine, sine], axis=1), last)):
        outs[2 * i][...], outs[2 * i + 1][...] = split2(table)
    turn_cos[...], turn_sin[...] = turn_c, turn_s
    squared = table_ref[tables_at[-1] :, :]
    cell = tile_ref[...] * PIX + pixel_ref[...]
    high = jnp.right_shift(cell, LOW.bit_length() - 1).astype(f32)
    low = jnp.bitwise_and(cell, LOW - 1).astype(f32)
    for lane in range(rows * HALVES):
        cols = slice(lane * LANES, (lane + 1) * LANES)
        start = (lane % HALVES * rows + lane // HALVES) * local_dets
        hi_s[start : start + local_dets, :] = high[:, cols]
        lo_s[start : start + local_dets, :] = low[:, cols]
    for det in range(local_dets):
        high_ref[det] = take_rows(hi_s, det, rows, local_dets)
        low_ref[det] = take_rows(lo_s, det, rows, local_dets)
        knee = knee_ref[det]
        gain_ref[det] = squared / (white_ref[det] * (squared + knee * knee))
        inverse_ref[det] = 1.0 / jnp.full((1, COLS), white_ref[det], f32)


def filter_kernel(parts, first_det, count, dets, final, order_ref, *refs):
    part_refs = refs[:parts]
    (f_h, f_l, s_h, s_l, l_h, l_l, tc_ref, ts_ref, gain_ref, inverse_ref, high_ref, low_ref) = refs[
        parts : parts + 12
    ]
    refs = refs[parts + 12 :]
    if first_det > 0:
        before_ref, sums_ref, refs = refs[0], refs[1], refs[2:]
    if final:
        out_ref, sky_ref, weight_ref, signal, stacked, totals = refs
    else:
        stacked, totals, signal = refs
    rows = signal.shape[0]
    half = rows // 2
    totals[...] = sums_ref[...] if first_det > 0 else jnp.zeros_like(totals)
    tall = totals.shape[0] // 2
    row_index = lax.broadcasted_iota(jnp.int32, (half, COLS), 0)
    chip = jnp.right_shift(lax.axis_index("tm"), 1)

    def one(turn):
        det = turn + first_det
        for part in range(parts):
            height = part_refs[part].shape[1]
            start = 0
            if parts > 1:
                start = pl.multiple_of(jnp.bitwise_xor(chip, part) * height, height)
            signal[pl.ds(start, height), :] = part_refs[part][turn]
        turn_cos, turn_sin = tc_ref[...], ts_ref[...]
        side = (s_h[...], s_l[...])
        first = dot3((f_h[...], f_l[...]), split2(signal[...]))
        real_y, low_y = first[:half], first[half:]
        imag_y = jnp.where(row_index == 0, 0.0, low_y)
        zero_y = jnp.broadcast_to(low_y[0:1], (16, COLS))
        real_z = real_y * turn_cos + imag_y * turn_sin
        imag_z = imag_y * turn_cos - real_y * turn_sin
        forward = dot3(split2(jnp.concatenate([real_z, imag_z, zero_y], axis=0)), side)
        cos_f, sin_f = forward[:, :COLS], forward[:, COLS:]
        gain = gain_ref[det]
        gain_main, gain_zero = gain[:half], gain[half:]
        real_x = (cos_f[:half] + sin_f[half : 2 * half]) * gain_main
        imag_x = (cos_f[half : 2 * half] - sin_f[:half]) * gain_main
        zero_r = cos_f[2 * half :] * gain_zero
        zero_i = -sin_f[2 * half :] * gain_zero
        back = dot3(split2(jnp.concatenate([real_x, imag_x, zero_r, zero_i], axis=0)), side)
        cos_b, sin_b = back[:, :COLS], back[:, COLS:]
        real_u = cos_b[:half] - sin_b[half : 2 * half]
        imag_u = sin_b[:half] + cos_b[half : 2 * half]
        zero_o = cos_b[2 * half : 2 * half + 16] - sin_b[2 * half + 16 :]
        real_v = real_u * turn_cos - imag_u * turn_sin
        imag_v = real_u * turn_sin + imag_u * turn_cos
        imag_v = jnp.where(row_index == 0, zero_o[0:1], imag_v)
        result = dot3((l_h[...], l_l[...]), split2(jnp.concatenate([real_v, imag_v], axis=0)))
        for half_index in range(HALVES):
            cols = slice(half_index * LANES, (half_index + 1) * LANES)
            stacked[pl.ds(half_index * rows * dets + det, rows, stride=dets), :] = result[:, cols]
        return result

    results = [one(turn) for turn in range(count)]
    if final:
        det_index = lax.broadcasted_iota(jnp.int32, (dets, LANES), 0)
        for lane in range(rows * HALVES):
            start = (lane % HALVES * rows + lane // HALVES) * dets
            here = stacked[start : start + dets, :]
            if first_det > 0:
                here = jnp.where(det_index < first_det, before_ref[start : start + dets, :], here)
            out_ref[:, lane * LANES : (lane + 1) * LANES] = here.astype(bf16)
    for turn, result in enumerate(results):
        det = turn + first_det
        totals[...] += binned(high_ref[det], low_ref[det], result, inverse_ref[det], tall)
    if final:
        per_tile = PIX // LOW
        for tile in range(sky_ref.shape[0]):
            source = order_ref[tile] * per_tile
            for piece in range(per_tile):
                cols = slice(piece * LOW, (piece + 1) * LOW)
                sky_ref[tile : tile + 1, cols] = totals[pl.ds(source + piece, 1), :]
                weight_ref[tile : tile + 1, cols] = totals[pl.ds(tall + source + piece, 1), :]


def swap(x, step, axis):
    size = lax.axis_size(axis)
    return lax.ppermute(x, axis, [(i, i ^ step) for i in range(size)])


def vmem(limit):
    return pltpu.CompilerParams(vmem_limit_bytes=limit * MIB)


def shards(
    detector_data, templates, wafer_of, knee_freq, white_level, tile_id, pixel_id, tile_order
):
    row_count, time_local = detector_data.shape
    wafer_count, modes, _ = templates.shape
    owners, groups = lax.axis_size("tm"), lax.axis_size("det")
    run_len = min(row_count, row_count * groups // wafer_count)
    runs = row_count // run_len
    width = runs * (modes + run_len)
    local_dets = row_count // owners
    full_length = time_local * owners
    rows = full_length // COLS
    pieces = time_local // COLS
    paired = owners & (owners - 1) == 0 and 4 <= owners <= 8 and run_len % (2 * local_dets) == 0
    step_len = min(STEP, time_local)
    smem = pl.BlockSpec(memory_space=pltpu.SMEM)
    whole = pl.BlockSpec(memory_space=pltpu.VMEM)
    anywhere = pl.BlockSpec(memory_space=pl.ANY)

    def template_spec(run):
        return pl.BlockSpec((1, modes, step_len), lambda i, w, run=run: (w[run * run_len], 0, i))

    def by_step(height):
        return pl.BlockSpec((height, step_len), lambda i, w: (0, i))

    if paired:
        got = swap(detector_data, 1, "tm")
    sums, *wide = pl.pallas_call(
        functools.partial(fit_kernel, runs, run_len, paired),
        out_shape=[jax.ShapeDtypeStruct((modes, width), f32)]
        + [jax.ShapeDtypeStruct((runs * modes, time_local), f32)] * paired,
        grid_spec=pltpu.PrefetchScalarGridSpec(
            num_scalar_prefetch=1,
            grid=(time_local // step_len,),
            in_specs=[by_step(row_count)] + [template_spec(run) for run in range(runs)],
            out_specs=[pl.BlockSpec((modes, width), lambda i, w: (0, 0))]
            + [by_step(runs * modes)] * paired,
        ),
        compiler_params=vmem(60),
        name="fit_sums",
    )(wafer_of, detector_data, *[templates] * runs)
    if paired:
        wide = swap(wide[0], 1, "tm")
    if paired:
        terms = [sums] + [swap(sums, step, "tm") for step in range(2, owners, 2)]
        while len(terms) > 1:
            terms = [a + b for a, b in zip(terms[0::2], terms[1::2])]
        sums = [terms[0], swap(terms[0], 1, "tm")]
    else:
        sums = [lax.psum(sums, "tm")]

    chunks = 2 if paired and local_dets % 2 == 0 else 1
    per_chunk = local_dets // chunks
    if paired:
        chips = owners // 2
        blocks_out = [(per_chunk, 2 * pieces, COLS)] * (chunks * chips)
        kernel = functools.partial(paired_kernel, runs, run_len, local_dets, chunks)
        operands = [detector_data, got, wide, templates]
        scratch = pltpu.VMEM((HALVES * pieces * row_count, LANES), f32)
    else:
        blocks_out = [(owners, local_dets, pieces, COLS)]
        kernel = functools.partial(residual_kernel, runs, run_len, owners)
        operands = [detector_data, templates]
        scratch = pltpu.VMEM((HALVES * pieces * row_count, LANES), f32)
    fit_amps, *blocks = pl.pallas_call(
        kernel,
        out_shape=[jax.ShapeDtypeStruct(shape, f32) for shape in [(modes, row_count), *blocks_out]],
        in_specs=[smem] + [whole] * (len(sums) + len(operands)),
        out_specs=[whole] * (1 + len(blocks_out)),
        scratch_shapes=[scratch],
        compiler_params=vmem(32),
        name="residual",
    )(wafer_of, *operands, *sums)

    if paired:
        received = [blocks[chunk * chips : (chunk + 1) * chips] for chunk in range(chunks)]
        for step in reversed(range(1, chips)):
            received[0][step] = swap(received[0][step], 2 * step, "tm")
    else:
        moved = lax.all_to_all(blocks[0], "tm", split_axis=0, concat_axis=0, tiled=True)
        received = [[jnp.swapaxes(moved, 0, 1).reshape(local_dets, rows, COLS)]]

    tile_count = tile_order.shape[0]
    tall = tile_count * PIX // LOW
    table = jnp.asarray(tables(rows))
    half = rows // 2
    grid_shape = (local_dets, rows, COLS)
    pair_shapes = [(rows, rows), (COLS, 2 * COLS), (rows, rows)]
    pairs = [jax.ShapeDtypeStruct(shape, bf16) for shape in pair_shapes for _ in range(2)]
    prepared_shapes = [
        (half, COLS),
        (half, COLS),
        (local_dets, half + 16, COLS),
        (local_dets, 1, COLS),
        grid_shape,
        grid_shape,
    ]
    prepared = pl.pallas_call(
        prepare_kernel,
        out_shape=pairs + [jax.ShapeDtypeStruct(shape, f32) for shape in prepared_shapes],
        in_specs=[smem, smem, anywhere, whole, whole, whole],
        out_specs=[whole] * 12,
        scratch_shapes=[pltpu.VMEM((HALVES * rows * local_dets, LANES), f32)] * 2,
        compiler_params=vmem(32),
        cost_estimate=pl.CostEstimate(
            flops=0, bytes_accessed=32 * local_dets * full_length, transcendentals=0
        ),
        name="prepare",
    )(knee_freq, white_level, fit_amps, table, tile_id, pixel_id)

    for chunk in range(1, chunks):
        near = [received[chunk - 1][:-1], received[chunk], prepared]
        near = lax.optimization_barrier(near)
        received[chunk - 1][:-1], received[chunk], prepared = near
        for step in reversed(range(1, chips)):
            received[chunk][step] = swap(received[chunk][step], 2 * step, "tm")

    stacked_shape = (HALVES * rows * local_dets, LANES)
    carried = []
    for chunk in range(chunks):
        final = chunk == chunks - 1
        first_det = chunk * per_chunk
        parts = len(received[chunk])
        if final:
            outs = [((local_dets, full_length), bf16)] + [((tile_count, PIX), f32)] * 2
            scratch = [pltpu.VMEM(s, f32) for s in ((rows, COLS), stacked_shape, (2 * tall, LOW))]
        else:
            outs = [(stacked_shape, f32), ((2 * tall, LOW), f32)]
            scratch = [pltpu.VMEM((rows, COLS), f32)]
        operands = [*received[chunk], *prepared, *carried]
        carried = pl.pallas_call(
            functools.partial(filter_kernel, parts, first_det, per_chunk, local_dets, final),
            out_shape=[jax.ShapeDtypeStruct(*o) for o in outs],
            in_specs=[smem] + [whole] * len(operands),
            out_specs=[whole] * len(outs),
            scratch_shapes=scratch,
            compiler_params=vmem(32),
            cost_estimate=pl.CostEstimate(
                flops=80000 * per_chunk * full_length,
                bytes_accessed=16 * per_chunk * full_length,
                transcendentals=0,
            ),
            name="filter_and_bin",
        )(tile_order, *operands)
    weighted_data, sky_part, weight_part = carried

    owned = tile_count * PIX // owners
    both = jnp.concatenate(
        [sky_part.reshape(owners, owned), weight_part.reshape(owners, owned)], axis=1
    )
    spread = jnp.broadcast_to(both[None], (groups, *both.shape)).reshape(groups * owners, 2 * owned)
    spread = lax.all_to_all(spread, ("det", "tm"), split_axis=0, concat_axis=0, tiled=True)
    scale = float(tile_count * PIX) / float(local_dets * groups * owners * full_length)
    summed = jnp.sum(spread, axis=0) * scale
    return (fit_amps, weighted_data, summed[:owned], summed[owned:])


def solution(mesh):
    in_specs = (
        P("det", "tm"),
        P(None, None, "tm"),
        P("det"),
        P(("det", "tm")),
        P(("det", "tm")),
        P(("det", "tm"), None),
        P(("det", "tm"), None),
        P(),
    )
    out_specs = (P(None, "det"), P(("det", "tm"), None), P("tm"), P("tm"))
    return jax.shard_map(shards, mesh=mesh, in_specs=in_specs, out_specs=out_specs, check_vma=False)
```

```python
import functools
import math

import jax
import jax.numpy as jnp
import numpy as np
from jax import lax
from jax.experimental import pallas as pl
from jax.experimental.pallas import tpu as pltpu
from jax.sharding import PartitionSpec as P

PIX = 128
COLS = 256
LANES = 128
HALVES = COLS // LANES
LOW = 64
SAMPLE_RATE = 200.0
MIB = 1024 * 1024
STEP = 8192
NT = (((1,), (1,)), ((), ()))
f32 = jnp.float32
bf16 = jnp.bfloat16


def split2(x):
    high = x.astype(bf16)
    return high, (x - high.astype(f32)).astype(bf16)


def split3(x):
    high = x.astype(bf16)
    rest = x - high.astype(f32)
    mid = rest.astype(bf16)
    return high, mid, (rest - mid.astype(f32)).astype(bf16)


@functools.lru_cache(maxsize=None)
def tables(rows):
    total = rows * COLS
    half = rows // 2
    slots = np.arange(half)
    slots[0] = half
    ramp = np.arange(rows)
    angle = 2.0 * np.pi * (slots[:, None] * ramp[None, :] % rows) / rows
    first = np.concatenate([np.cos(angle), -np.sin(angle)], axis=0)
    first[half] = 1.0
    weight = np.full((half,), 2.0)
    weight[0] = 1.0
    last = np.concatenate([weight[:, None] * np.cos(angle), -2.0 * np.sin(angle)], axis=0)
    last[half] = 1.0
    last = last.T / total
    col = np.arange(COLS)
    phase = 2.0 * np.pi * (col[:, None] * col[None, :] % COLS) / COLS
    turn = 2.0 * np.pi * (slots[:, None] * col[None, :] % total) / total
    bins = np.concatenate([slots, np.zeros((16,), np.int64)])[:, None] + rows * col[None, :]
    freq = np.minimum(bins, total - bins).astype(np.float32) * np.float32(SAMPLE_RATE / total)
    made = [first, np.cos(phase), np.sin(phase), last, np.cos(turn), np.sin(turn), freq * freq]
    return np.concatenate([table.astype(np.float32) for table in made], axis=0)


def dot3(left, right):
    (lh, ll), (rh, rl) = left, right
    return jnp.dot(
        jnp.concatenate([lh, ll, lh], axis=1),
        jnp.concatenate([rh, rh, rl], axis=0),
        preferred_element_type=f32,
    )


def fit_kernel(runs, run_len, paired, wafer_ref, data_ref, *refs):
    template_refs, out_ref = refs[:runs], refs[runs]
    parts = []
    for run in range(runs):
        temp = template_refs[run][0]
        modes = temp.shape[0]
        high, mid, low = split3(data_ref[run * run_len : (run + 1) * run_len, :])
        both = lax.dot_general(
            temp, jnp.concatenate([temp, high, mid, low], axis=0), NT, preferred_element_type=f32
        )
        ends = [modes + i * run_len for i in range(4)]
        parts.append(both[:, :modes])
        parts.append(
            both[:, ends[0] : ends[1]] + both[:, ends[1] : ends[2]] + both[:, ends[2] : ends[3]]
        )
        if paired:
            refs[runs + 1][run * modes : (run + 1) * modes, :] = temp.astype(f32)
    part = jnp.concatenate(parts, axis=1)

    @pl.when(pl.program_id(0) == 0)
    def _():
        out_ref[...] = part

    @pl.when(pl.program_id(0) > 0)
    def _():
        out_ref[...] += part


def eliminate(sums, runs, run_len, modes):
    width = modes + run_len
    row_index = lax.broadcasted_iota(jnp.int32, (modes, width), 0)
    joined = [sums[:, run * width : (run + 1) * width] for run in range(runs)]
    for column in range(modes):
        for run in range(runs):
            now = joined[run]
            pivot_row = now[column : column + 1, :] / now[column : column + 1, column : column + 1]
            rest = now - now[:, column : column + 1] * pivot_row
            joined[run] = jnp.where(row_index == column, pivot_row, rest)
    return [now[:, modes:] for now in joined]


def paired_kernel(
    runs, run_len, local_dets, chunks, wafer_ref, data_ref, got_ref, wide_ref, temp_ref, *refs
):
    chips = data_ref.shape[0] // (2 * local_dets)
    sums, refs = refs[0][...] + refs[1][...], refs[2:]
    amps_ref, out_refs, rows_ref = refs[0], refs[1:-1], refs[-1]
    modes = temp_ref.shape[1]
    row_count, time_local = data_ref.shape
    kept = row_count // 2
    pieces = time_local // COLS
    amps = eliminate(sums, runs, run_len, modes)
    amps_ref[...] = jnp.concatenate(amps, axis=1)
    me = lax.axis_index("tm")
    core, chip = jnp.bitwise_and(me, 1), jnp.right_shift(me, 1)
    per_run = run_len // 2
    shard_rows = HALVES * pieces * kept

    def mine(rows):
        groups = [rows[start : start + local_dets] for start in range(0, run_len, local_dets)]
        even, odd = jnp.concatenate(groups[0::2], axis=0), jnp.concatenate(groups[1::2], axis=0)
        return jnp.where(core == 0, even, odd)

    for run in range(runs):
        left = jnp.concatenate(split3(mine(amps[run].T)), axis=1)
        own = temp_ref[wafer_ref[run * run_len]]
        other = wide_ref[run * modes : (run + 1) * modes, :].astype(bf16)
        for side, (temp, source) in enumerate([(own, data_ref), (other, got_ref)]):
            fitted = jnp.dot(left, jnp.concatenate([temp] * 3, axis=0), preferred_element_type=f32)
            kept_rows = mine(source[run * run_len : (run + 1) * run_len, :]) - fitted
            for lane in range(time_local // LANES):
                start = side * shard_rows + run * per_run
                start += (lane % HALVES * pieces + lane // HALVES) * kept
                rows_ref[start : start + per_run, :] = kept_rows[:, lane * LANES : (lane + 1) * LANES]
    per_chunk = local_dets // chunks
    for chunk in range(chunks):
        for step in range(chips):
            base = jnp.bitwise_xor(chip, step) * local_dets + chunk * per_chunk
            for det in range(per_chunk):
                for side in range(2):
                    place = pl.multiple_of(jnp.bitwise_xor(core, side) * pieces, pieces)
                    out_refs[chunk * chips + step][det, pl.ds(place, pieces), :] = take_rows(
                        rows_ref, side * shard_rows + base + det, pieces, kept
                    )


def residual_kernel(runs, run_len, owners, wafer_ref, data_ref, temp_ref, sums_ref, *refs):
    amps_ref, out_ref, rows_ref = refs
    modes = temp_ref.shape[1]
    row_count, time_local = data_ref.shape
    pieces = time_local // COLS
    amps = eliminate(sums_ref[...], runs, run_len, modes)
    amps_ref[...] = jnp.concatenate(amps, axis=1)
    for run in range(runs):
        temp = temp_ref[wafer_ref[run * run_len]]
        left = jnp.concatenate(split3(amps[run].T), axis=1)
        fitted = jnp.dot(left, jnp.concatenate([temp] * 3, axis=0), preferred_element_type=f32)
        rows = slice(run * run_len, (run + 1) * run_len)
        for lane in range(time_local // LANES):
            cols = slice(lane * LANES, (lane + 1) * LANES)
            start = (lane % HALVES * pieces + lane // HALVES) * row_count + run * run_len
            rows_ref[start : start + run_len, :] = data_ref[rows, cols] - fitted[:, cols]
    local_dets = row_count // owners
    for owner in range(owners):
        for det in range(local_dets):
            out_ref[owner, det] = take_rows(rows_ref, owner * local_dets + det, pieces, row_count)


def take_rows(ref, start, count, stride):
    return jnp.concatenate(
        [
            ref[pl.ds(side * count * stride + start, count, stride=stride), :]
            for side in range(HALVES)
        ],
        axis=1,
    )


def binned(high_rows, low_rows, value_rows, weight_row, tall):
    high_ramp = lax.broadcasted_iota(jnp.int32, (tall, COLS), 0).astype(f32).astype(bf16)
    low_ramp = lax.broadcasted_iota(jnp.int32, (LOW, COLS), 0).astype(f32).astype(bf16)
    weight = jnp.broadcast_to(weight_row, (tall, COLS)).astype(bf16)
    zero, one = jnp.zeros((tall, COLS), bf16), jnp.ones((LOW, COLS), bf16)
    lefts, rights = [], []
    for row in range(high_rows.shape[0]):
        high = jnp.broadcast_to(high_rows[row : row + 1], (tall, COLS)).astype(bf16)
        low = jnp.broadcast_to(low_rows[row : row + 1], (LOW, COLS)).astype(bf16)
        value = jnp.broadcast_to(value_rows[row : row + 1], (tall, COLS)).astype(bf16)
        hot = high == high_ramp
        lefts.append(
            jnp.concatenate([jnp.where(hot, value, zero), jnp.where(hot, weight, zero)], axis=0)
        )
        rights.append(jnp.where(low == low_ramp, one, jnp.zeros_like(one)))
    return lax.dot_general(
        jnp.concatenate(lefts, axis=1),
        jnp.concatenate(rights, axis=1),
        NT,
        preferred_element_type=f32,
    )


def prepare_kernel(knee_ref, white_ref, after_ref, table_ref, tile_ref, pixel_ref, *refs):
    outs, (turn_cos, turn_sin, gain_ref, inverse_ref, high_ref, low_ref, hi_s, lo_s) = refs[:6], refs[6:]
    local_dets, rows = high_ref.shape[0], high_ref.shape[1]
    half = rows // 2
    tables_at = [0]
    for height in (rows, COLS, COLS, rows, half, half):
        tables_at.append(tables_at[-1] + height)
    first, cosine, sine, last, turn_c, turn_s = (
        table_ref[start:end, :] for start, end in zip(tables_at[:-1], tables_at[1:])
    )
    for i, table in enumerate((first, jnp.concatenate([cosine, sine], axis=1), last)):
        outs[2 * i][...], outs[2 * i + 1][...] = split2(table)
    turn_cos[...], turn_sin[...] = turn_c, turn_s
    squared = table_ref[tables_at[-1] :, :]
    cell = tile_ref[...] * PIX + pixel_ref[...]
    high = jnp.right_shift(cell, LOW.bit_length() - 1).astype(f32)
    low = jnp.bitwise_and(cell, LOW - 1).astype(f32)
    for lane in range(rows * HALVES):
        cols = slice(lane * LANES, (lane + 1) * LANES)
        start = (lane % HALVES * rows + lane // HALVES) * local_dets
        hi_s[start : start + local_dets, :] = high[:, cols]
        lo_s[start : start + local_dets, :] = low[:, cols]
    for det in range(local_dets):
        high_ref[det] = take_rows(hi_s, det, rows, local_dets)
        low_ref[det] = take_rows(lo_s, det, rows, local_dets)
        knee = knee_ref[det]
        gain_ref[det] = squared / (white_ref[det] * (squared + knee * knee))
        inverse_ref[det] = 1.0 / jnp.full((1, COLS), white_ref[det], f32)


def filter_kernel(parts, first_det, count, dets, final, order_ref, *refs):
    part_refs = refs[:parts]
    (f_h, f_l, s_h, s_l, l_h, l_l, tc_ref, ts_ref, gain_ref, inverse_ref, high_ref, low_ref) = refs[
        parts : parts + 12
    ]
    refs = refs[parts + 12 :]
    if first_det > 0:
        before_ref, sums_ref, refs = refs[0], refs[1], refs[2:]
    if final:
        out_ref, sky_ref, weight_ref, signal, stacked, totals = refs
    else:
        stacked, totals, signal = refs
    rows = signal.shape[0]
    half = rows // 2
    totals[...] = sums_ref[...] if first_det > 0 else jnp.zeros_like(totals)
    tall = totals.shape[0] // 2
    row_index = lax.broadcasted_iota(jnp.int32, (half, COLS), 0)
    chip = jnp.right_shift(lax.axis_index("tm"), 1)

    turn_cos, turn_sin = tc_ref[...], ts_ref[...]
    side = (s_h[...], s_l[...])
    turns = range(count)
    slabs = []
    for turn in turns:
        for part in range(parts):
            height = part_refs[part].shape[1]
            start = 0
            if parts > 1:
                start = pl.multiple_of(jnp.bitwise_xor(chip, part) * height, height)
            signal[pl.ds(start, height), turn * COLS : (turn + 1) * COLS] = part_refs[part][turn]
    first = dot3((f_h[...], f_l[...]), split2(signal[...]))
    for turn in turns:
        cols = slice(turn * COLS, (turn + 1) * COLS)
        real_y, low_y = first[:half, cols], first[half:, cols]
        imag_y = jnp.where(row_index == 0, 0.0, low_y)
        slabs.append(real_y * turn_cos + imag_y * turn_sin)
        slabs.append(imag_y * turn_cos - real_y * turn_sin)
        slabs.append(jnp.broadcast_to(low_y[0:1], (16, COLS)))
    forward = dot3(split2(jnp.concatenate(slabs, axis=0)), side)
    height = 2 * half + 16
    slabs = []
    for turn in turns:
        cos_f = forward[turn * height : (turn + 1) * height, :COLS]
        sin_f = forward[turn * height : (turn + 1) * height, COLS:]
        gain = gain_ref[turn + first_det]
        gain_main, gain_zero = gain[:half], gain[half:]
        slabs.append((cos_f[:half] + sin_f[half : 2 * half]) * gain_main)
        slabs.append((cos_f[half : 2 * half] - sin_f[:half]) * gain_main)
        slabs.append(cos_f[2 * half :] * gain_zero)
        slabs.append(-sin_f[2 * half :] * gain_zero)
    back = dot3(split2(jnp.concatenate(slabs, axis=0)), side)
    height = 2 * half + 32
    slabs = []
    for turn in turns:
        cos_b = back[turn * height : (turn + 1) * height, :COLS]
        sin_b = back[turn * height : (turn + 1) * height, COLS:]
        real_u = cos_b[:half] - sin_b[half : 2 * half]
        imag_u = sin_b[:half] + cos_b[half : 2 * half]
        zero_o = cos_b[2 * half : 2 * half + 16] - sin_b[2 * half + 16 :]
        imag_v = real_u * turn_sin + imag_u * turn_cos
        imag_v = jnp.where(row_index == 0, zero_o[0:1], imag_v)
        slabs.append(jnp.concatenate([real_u * turn_cos - imag_u * turn_sin, imag_v], axis=0))
    result = dot3((l_h[...], l_l[...]), split2(jnp.concatenate(slabs, axis=1)))
    results = [result[:, turn * COLS : (turn + 1) * COLS] for turn in turns]
    for turn in turns:
        for half_index in range(HALVES):
            cols = slice(half_index * LANES, (half_index + 1) * LANES)
            start = half_index * rows * dets + first_det + turn
            stacked[pl.ds(start, rows, stride=dets), :] = results[turn][:, cols]
    if final:
        det_index = lax.broadcasted_iota(jnp.int32, (dets, LANES), 0)
        for lane in range(rows * HALVES):
            start = (lane % HALVES * rows + lane // HALVES) * dets
            here = stacked[start : start + dets, :]
            if first_det > 0:
                here = jnp.where(det_index < first_det, before_ref[start : start + dets, :], here)
            out_ref[:, lane * LANES : (lane + 1) * LANES] = here.astype(bf16)
    for turn, result in enumerate(results):
        det = turn + first_det
        totals[...] += binned(high_ref[det], low_ref[det], result, inverse_ref[det], tall)
    if final:
        per_tile = PIX // LOW
        for tile in range(sky_ref.shape[0]):
            source = order_ref[tile] * per_tile
            for piece in range(per_tile):
                cols = slice(piece * LOW, (piece + 1) * LOW)
                sky_ref[tile : tile + 1, cols] = totals[pl.ds(source + piece, 1), :]
                weight_ref[tile : tile + 1, cols] = totals[pl.ds(tall + source + piece, 1), :]


def swap(x, step, axis):
    size = lax.axis_size(axis)
    return lax.ppermute(x, axis, [(i, i ^ step) for i in range(size)])


def vmem(limit):
    return pltpu.CompilerParams(vmem_limit_bytes=limit * MIB)


def shards(
    detector_data, templates, wafer_of, knee_freq, white_level, tile_id, pixel_id, tile_order
):
    row_count, time_local = detector_data.shape
    wafer_count, modes, _ = templates.shape
    owners, groups = lax.axis_size("tm"), lax.axis_size("det")
    run_len = min(row_count, row_count * groups // wafer_count)
    runs = row_count // run_len
    width = runs * (modes + run_len)
    local_dets = row_count // owners
    full_length = time_local * owners
    rows = full_length // COLS
    pieces = time_local // COLS
    paired = owners & (owners - 1) == 0 and 4 <= owners <= 8 and run_len % (2 * local_dets) == 0
    step_len = min(STEP, time_local)
    smem = pl.BlockSpec(memory_space=pltpu.SMEM)
    whole = pl.BlockSpec(memory_space=pltpu.VMEM)
    anywhere = pl.BlockSpec(memory_space=pl.ANY)

    def template_spec(run):
        return pl.BlockSpec((1, modes, step_len), lambda i, w, run=run: (w[run * run_len], 0, i))

    def by_step(height):
        return pl.BlockSpec((height, step_len), lambda i, w: (0, i))

    if paired:
        got = swap(detector_data, 1, "tm")
    sums, *wide = pl.pallas_call(
        functools.partial(fit_kernel, runs, run_len, paired),
        out_shape=[jax.ShapeDtypeStruct((modes, width), f32)]
        + [jax.ShapeDtypeStruct((runs * modes, time_local), f32)] * paired,
        grid_spec=pltpu.PrefetchScalarGridSpec(
            num_scalar_prefetch=1,
            grid=(time_local // step_len,),
            in_specs=[by_step(row_count)] + [template_spec(run) for run in range(runs)],
            out_specs=[pl.BlockSpec((modes, width), lambda i, w: (0, 0))]
            + [by_step(runs * modes)] * paired,
        ),
        compiler_params=vmem(60),
        name="fit_sums",
    )(wafer_of, detector_data, *[templates] * runs)
    if paired:
        wide = swap(wide[0], 1, "tm")
    if paired:
        terms = [sums] + [swap(sums, step, "tm") for step in range(2, owners, 2)]
        while len(terms) > 1:
            terms = [a + b for a, b in zip(terms[0::2], terms[1::2])]
        sums = [terms[0], swap(terms[0], 1, "tm")]
    else:
        sums = [lax.psum(sums, "tm")]

    chunks = 2 if paired and local_dets % 2 == 0 else 1
    per_chunk = local_dets // chunks
    if paired:
        chips = owners // 2
        blocks_out = [(per_chunk, 2 * pieces, COLS)] * (chunks * chips)
        kernel = functools.partial(paired_kernel, runs, run_len, local_dets, chunks)
        operands = [detector_data, got, wide, templates]
        scratch = pltpu.VMEM((HALVES * pieces * row_count, LANES), f32)
    else:
        blocks_out = [(owners, local_dets, pieces, COLS)]
        kernel = functools.partial(residual_kernel, runs, run_len, owners)
        operands = [detector_data, templates]
        scratch = pltpu.VMEM((HALVES * pieces * row_count, LANES), f32)
    fit_amps, *blocks = pl.pallas_call(
        kernel,
        out_shape=[jax.ShapeDtypeStruct(shape, f32) for shape in [(modes, row_count), *blocks_out]],
        in_specs=[smem] + [whole] * (len(sums) + len(operands)),
        out_specs=[whole] * (1 + len(blocks_out)),
        scratch_shapes=[scratch],
        compiler_params=vmem(32),
        name="residual",
    )(wafer_of, *operands, *sums)

    if paired:
        received = [blocks[chunk * chips : (chunk + 1) * chips] for chunk in range(chunks)]
        for step in reversed(range(1, chips)):
            received[0][step] = swap(received[0][step], 2 * step, "tm")
    else:
        moved = lax.all_to_all(blocks[0], "tm", split_axis=0, concat_axis=0, tiled=True)
        received = [[jnp.swapaxes(moved, 0, 1).reshape(local_dets, rows, COLS)]]

    tile_count = tile_order.shape[0]
    tall = tile_count * PIX // LOW
    table = jnp.asarray(tables(rows))
    half = rows // 2
    grid_shape = (local_dets, rows, COLS)
    pair_shapes = [(rows, rows), (COLS, 2 * COLS), (rows, rows)]
    pairs = [jax.ShapeDtypeStruct(shape, bf16) for shape in pair_shapes for _ in range(2)]
    prepared_shapes = [
        (half, COLS),
        (half, COLS),
        (local_dets, half + 16, COLS),
        (local_dets, 1, COLS),
        grid_shape,
        grid_shape,
    ]
    prepared = pl.pallas_call(
        prepare_kernel,
        out_shape=pairs + [jax.ShapeDtypeStruct(shape, f32) for shape in prepared_shapes],
        in_specs=[smem, smem, anywhere, whole, whole, whole],
        out_specs=[whole] * 12,
        scratch_shapes=[pltpu.VMEM((HALVES * rows * local_dets, LANES), f32)] * 2,
        compiler_params=vmem(32),
        cost_estimate=pl.CostEstimate(
            flops=0, bytes_accessed=32 * local_dets * full_length, transcendentals=0
        ),
        name="prepare",
    )(knee_freq, white_level, fit_amps, table, tile_id, pixel_id)

    for chunk in range(1, chunks):
        near = [received[chunk - 1][:-1], received[chunk], prepared]
        near = lax.optimization_barrier(near)
        received[chunk - 1][:-1], received[chunk], prepared = near
        for step in reversed(range(1, chips)):
            received[chunk][step] = swap(received[chunk][step], 2 * step, "tm")

    stacked_shape = (HALVES * rows * local_dets, LANES)
    carried = []
    for chunk in range(chunks):
        final = chunk == chunks - 1
        first_det = chunk * per_chunk
        parts = len(received[chunk])
        if final:
            outs = [((local_dets, full_length), bf16)] + [((tile_count, PIX), f32)] * 2
            scratch = [pltpu.VMEM(s, f32) for s in ((rows, per_chunk * COLS), stacked_shape, (2 * tall, LOW))]
        else:
            outs = [(stacked_shape, f32), ((2 * tall, LOW), f32)]
            scratch = [pltpu.VMEM((rows, per_chunk * COLS), f32)]
        operands = [*received[chunk], *prepared, *carried]
        carried = pl.pallas_call(
            functools.partial(filter_kernel, parts, first_det, per_chunk, local_dets, final),
            out_shape=[jax.ShapeDtypeStruct(*o) for o in outs],
            in_specs=[smem] + [whole] * len(operands),
            out_specs=[whole] * len(outs),
            scratch_shapes=scratch,
            compiler_params=vmem(32),
            cost_estimate=pl.CostEstimate(
                flops=80000 * per_chunk * full_length,
                bytes_accessed=16 * per_chunk * full_length,
                transcendentals=0,
            ),
            name="filter_and_bin",
        )(tile_order, *operands)
    weighted_data, sky_part, weight_part = carried

    owned = tile_count * PIX // owners
    both = jnp.concatenate(
        [sky_part.reshape(owners, owned), weight_part.reshape(owners, owned)], axis=1
    )
    spread = jnp.broadcast_to(both[None], (groups, *both.shape)).reshape(groups * owners, 2 * owned)
    spread = lax.all_to_all(spread, ("det", "tm"), split_axis=0, concat_axis=0, tiled=True)
    scale = float(tile_count * PIX) / float(local_dets * groups * owners * full_length)
    summed = jnp.sum(spread, axis=0) * scale
    return (fit_amps, weighted_data, summed[:owned], summed[owned:])


def solution(mesh):
    in_specs = (
        P("det", "tm"),
        P(None, None, "tm"),
        P("det"),
        P(("det", "tm")),
        P(("det", "tm")),
        P(("det", "tm"), None),
        P(("det", "tm"), None),
        P(),
    )
    out_specs = (P(None, "det"), P(("det", "tm"), None), P("tm"), P("tm"))
    return jax.shard_map(shards, mesh=mesh, in_specs=in_specs, out_specs=out_specs, check_vma=False)
```

```python
import functools
import math

import jax
import jax.numpy as jnp
import numpy as np
from jax import lax
from jax.experimental import pallas as pl
from jax.experimental.pallas import tpu as pltpu
from jax.sharding import PartitionSpec as P

PIX = 128
COLS = 256
LANES = 128
HALVES = COLS // LANES
LOW = 64
SAMPLE_RATE = 200.0
MIB = 1024 * 1024
STEP = 8192
NT = (((1,), (1,)), ((), ()))
f32 = jnp.float32
bf16 = jnp.bfloat16


def split2(x):
    high = x.astype(bf16)
    return high, (x - high.astype(f32)).astype(bf16)


def split3(x):
    high = x.astype(bf16)
    rest = x - high.astype(f32)
    mid = rest.astype(bf16)
    return high, mid, (rest - mid.astype(f32)).astype(bf16)


@functools.lru_cache(maxsize=None)
def tables(rows):
    total = rows * COLS
    half = rows // 2
    slots = np.arange(half)
    slots[0] = half
    ramp = np.arange(rows)
    angle = 2.0 * np.pi * (slots[:, None] * ramp[None, :] % rows) / rows
    first = np.concatenate([np.cos(angle), -np.sin(angle)], axis=0)
    first[half] = 1.0
    weight = np.full((half,), 2.0)
    weight[0] = 1.0
    last = np.concatenate([weight[:, None] * np.cos(angle), -2.0 * np.sin(angle)], axis=0)
    last[half] = 1.0
    last = last.T / total
    col = np.arange(COLS)
    phase = 2.0 * np.pi * (col[:, None] * col[None, :] % COLS) / COLS
    turn = 2.0 * np.pi * (slots[:, None] * col[None, :] % total) / total
    bins = np.concatenate([slots, np.zeros((16,), np.int64)])[:, None] + rows * col[None, :]
    freq = np.minimum(bins, total - bins).astype(np.float32) * np.float32(SAMPLE_RATE / total)
    made = [first, np.cos(phase), np.sin(phase), last, np.cos(turn), np.sin(turn), freq * freq]
    return np.concatenate([table.astype(np.float32) for table in made], axis=0)


def dot3(left, right):
    (lh, ll), (rh, rl) = left, right
    return jnp.dot(
        jnp.concatenate([lh, ll, lh], axis=1),
        jnp.concatenate([rh, rh, rl], axis=0),
        preferred_element_type=f32,
    )


def fit_kernel(runs, run_len, paired, wafer_ref, data_ref, *refs):
    template_refs, out_ref = refs[:runs], refs[runs]
    parts = []
    for run in range(runs):
        temp = template_refs[run][0]
        modes = temp.shape[0]
        high, mid, low = split3(data_ref[run * run_len : (run + 1) * run_len, :])
        both = lax.dot_general(
            temp, jnp.concatenate([temp, high, mid, low], axis=0), NT, preferred_element_type=f32
        )
        ends = [modes + i * run_len for i in range(4)]
        parts.append(both[:, :modes])
        parts.append(
            both[:, ends[0] : ends[1]] + both[:, ends[1] : ends[2]] + both[:, ends[2] : ends[3]]
        )
        if paired:
            refs[runs + 1][run * modes : (run + 1) * modes, :] = temp.astype(f32)
    part = jnp.concatenate(parts, axis=1)

    @pl.when(pl.program_id(0) == 0)
    def _():
        out_ref[...] = part

    @pl.when(pl.program_id(0) > 0)
    def _():
        out_ref[...] += part


def eliminate(sums, runs, run_len, modes):
    width = modes + run_len
    row_index = lax.broadcasted_iota(jnp.int32, (modes, width), 0)
    joined = [sums[:, run * width : (run + 1) * width] for run in range(runs)]
    for column in range(modes):
        for run in range(runs):
            now = joined[run]
            pivot_row = now[column : column + 1, :] / now[column : column + 1, column : column + 1]
            rest = now - now[:, column : column + 1] * pivot_row
            joined[run] = jnp.where(row_index == column, pivot_row, rest)
    return [now[:, modes:] for now in joined]


def paired_kernel(
    runs, run_len, local_dets, chunks, wafer_ref, data_ref, got_ref, wide_ref, temp_ref, *refs
):
    chips = data_ref.shape[0] // (2 * local_dets)
    sums, refs = refs[0][...] + refs[1][...], refs[2:]
    amps_ref, out_refs, rows_ref = refs[0], refs[1:-1], refs[-1]
    modes = temp_ref.shape[1]
    row_count, time_local = data_ref.shape
    kept = row_count // 2
    pieces = time_local // COLS
    amps = eliminate(sums, runs, run_len, modes)
    amps_ref[...] = jnp.concatenate(amps, axis=1)
    me = lax.axis_index("tm")
    core, chip = jnp.bitwise_and(me, 1), jnp.right_shift(me, 1)
    per_run = run_len // 2
    shard_rows = HALVES * pieces * kept

    def mine(rows):
        groups = [rows[start : start + local_dets] for start in range(0, run_len, local_dets)]
        even, odd = jnp.concatenate(groups[0::2], axis=0), jnp.concatenate(groups[1::2], axis=0)
        return jnp.where(core == 0, even, odd)

    for run in range(runs):
        left = jnp.concatenate(split3(mine(amps[run].T)), axis=1)
        own = temp_ref[wafer_ref[run * run_len]]
        other = wide_ref[run * modes : (run + 1) * modes, :].astype(bf16)
        for side, (temp, source) in enumerate([(own, data_ref), (other, got_ref)]):
            fitted = jnp.dot(left, jnp.concatenate([temp] * 3, axis=0), preferred_element_type=f32)
            kept_rows = mine(source[run * run_len : (run + 1) * run_len, :]) - fitted
            for lane in range(time_local // LANES):
                start = side * shard_rows + run * per_run
                start += (lane % HALVES * pieces + lane // HALVES) * kept
                rows_ref[start : start + per_run, :] = kept_rows[:, lane * LANES : (lane + 1) * LANES]
    per_chunk = local_dets // chunks
    for chunk in range(chunks):
        for step in range(chips):
            base = jnp.bitwise_xor(chip, step) * local_dets + chunk * per_chunk
            for det in range(per_chunk):
                for side in range(2):
                    place = pl.multiple_of(jnp.bitwise_xor(core, side) * pieces, pieces)
                    out_refs[chunk * chips + step][det, pl.ds(place, pieces), :] = take_rows(
                        rows_ref, side * shard_rows + base + det, pieces, kept
                    )


def residual_kernel(runs, run_len, owners, wafer_ref, data_ref, temp_ref, sums_ref, *refs):
    amps_ref, out_ref, rows_ref = refs
    modes = temp_ref.shape[1]
    row_count, time_local = data_ref.shape
    pieces = time_local // COLS
    amps = eliminate(sums_ref[...], runs, run_len, modes)
    amps_ref[...] = jnp.concatenate(amps, axis=1)
    for run in range(runs):
        temp = temp_ref[wafer_ref[run * run_len]]
        left = jnp.concatenate(split3(amps[run].T), axis=1)
        fitted = jnp.dot(left, jnp.concatenate([temp] * 3, axis=0), preferred_element_type=f32)
        rows = slice(run * run_len, (run + 1) * run_len)
        for lane in range(time_local // LANES):
            cols = slice(lane * LANES, (lane + 1) * LANES)
            start = (lane % HALVES * pieces + lane // HALVES) * row_count + run * run_len
            rows_ref[start : start + run_len, :] = data_ref[rows, cols] - fitted[:, cols]
    local_dets = row_count // owners
    for owner in range(owners):
        for det in range(local_dets):
            out_ref[owner, det] = take_rows(rows_ref, owner * local_dets + det, pieces, row_count)


def take_rows(ref, start, count, stride):
    return jnp.concatenate(
        [
            ref[pl.ds(side * count * stride + start, count, stride=stride), :]
            for side in range(HALVES)
        ],
        axis=1,
    )


def binned(high_rows, low_rows, value_rows, weight_row, tall):
    high_ramp = lax.broadcasted_iota(jnp.int32, (tall, COLS), 0).astype(f32).astype(bf16)
    low_ramp = lax.broadcasted_iota(jnp.int32, (LOW, COLS), 0).astype(f32).astype(bf16)
    weight = jnp.broadcast_to(weight_row, (tall, COLS)).astype(bf16)
    zero, one = jnp.zeros((tall, COLS), bf16), jnp.ones((LOW, COLS), bf16)
    lefts, rights = [], []
    for row in range(high_rows.shape[0]):
        high = jnp.broadcast_to(high_rows[row : row + 1], (tall, COLS)).astype(bf16)
        low = jnp.broadcast_to(low_rows[row : row + 1], (LOW, COLS)).astype(bf16)
        value = jnp.broadcast_to(value_rows[row : row + 1], (tall, COLS)).astype(bf16)
        hot = high == high_ramp
        lefts.append(
            jnp.concatenate([jnp.where(hot, value, zero), jnp.where(hot, weight, zero)], axis=0)
        )
        rights.append(jnp.where(low == low_ramp, one, jnp.zeros_like(one)))
    return lax.dot_general(
        jnp.concatenate(lefts, axis=1),
        jnp.concatenate(rights, axis=1),
        NT,
        preferred_element_type=f32,
    )


def prepare_kernel(knee_ref, white_ref, after_ref, table_ref, tile_ref, pixel_ref, *refs):
    outs, (turn_cos, turn_sin, gain_ref, inverse_ref, high_ref, low_ref, hi_s, lo_s) = refs[:6], refs[6:]
    local_dets, rows = high_ref.shape[0], high_ref.shape[1]
    half = rows // 2
    tables_at = [0]
    for height in (rows, COLS, COLS, rows, half, half):
        tables_at.append(tables_at[-1] + height)
    first, cosine, sine, last, turn_c, turn_s = (
        table_ref[start:end, :] for start, end in zip(tables_at[:-1], tables_at[1:])
    )
    for i, table in enumerate((first, jnp.concatenate([cosine, sine], axis=1), last)):
        outs[2 * i][...], outs[2 * i + 1][...] = split2(table)
    turn_cos[...], turn_sin[...] = turn_c, turn_s
    squared = table_ref[tables_at[-1] :, :]
    cell = tile_ref[...] * PIX + pixel_ref[...]
    high = jnp.right_shift(cell, LOW.bit_length() - 1).astype(f32)
    low = jnp.bitwise_and(cell, LOW - 1).astype(f32)
    for lane in range(rows * HALVES):
        cols = slice(lane * LANES, (lane + 1) * LANES)
        start = (lane % HALVES * rows + lane // HALVES) * local_dets
        hi_s[start : start + local_dets, :] = high[:, cols]
        lo_s[start : start + local_dets, :] = low[:, cols]
    for det in range(local_dets):
        high_ref[det] = take_rows(hi_s, det, rows, local_dets)
        low_ref[det] = take_rows(lo_s, det, rows, local_dets)
        knee = knee_ref[det]
        gain_ref[det] = squared / (white_ref[det] * (squared + knee * knee))
        inverse_ref[det] = 1.0 / jnp.full((1, COLS), white_ref[det], f32)


def filter_kernel(parts, first_det, count, dets, final, order_ref, *refs):
    part_refs = refs[:parts]
    (f_h, f_l, s_h, s_l, l_h, l_l, tc_ref, ts_ref, gain_ref, inverse_ref, high_ref, low_ref) = refs[
        parts : parts + 12
    ]
    refs = refs[parts + 12 :]
    if first_det > 0:
        before_ref, sums_ref, refs = refs[0], refs[1], refs[2:]
    if final:
        out_ref, sky_ref, weight_ref, signal, stacked, totals = refs
    else:
        stacked, totals, signal = refs
    rows = signal.shape[0]
    half = rows // 2
    totals[...] = sums_ref[...] if first_det > 0 else jnp.zeros_like(totals)
    tall = totals.shape[0] // 2
    row_index = lax.broadcasted_iota(jnp.int32, (half, COLS), 0)
    chip = jnp.right_shift(lax.axis_index("tm"), 1)

    turn_cos, turn_sin = tc_ref[...], ts_ref[...]
    side = (s_h[...], s_l[...])
    turns = range(count)
    slabs = []
    for turn in turns:
        for part in range(parts):
            height = part_refs[part].shape[1]
            start = 0
            if parts > 1:
                start = pl.multiple_of(jnp.bitwise_xor(chip, part) * height, height)
            signal[pl.ds(start, height), turn * COLS : (turn + 1) * COLS] = part_refs[part][turn]
    first = dot3((f_h[...], f_l[...]), split2(signal[...]))
    for turn in turns:
        cols = slice(turn * COLS, (turn + 1) * COLS)
        real_y, low_y = first[:half, cols], first[half:, cols]
        imag_y = jnp.where(row_index == 0, 0.0, low_y)
        slabs.append(real_y * turn_cos + imag_y * turn_sin)
        slabs.append(imag_y * turn_cos - real_y * turn_sin)
        slabs.append(jnp.broadcast_to(low_y[0:1], (16, COLS)))
    forward = dot3(split2(jnp.concatenate(slabs, axis=0)), side)
    height = 2 * half + 16
    slabs = []
    for turn in turns:
        cos_f = forward[turn * height : (turn + 1) * height, :COLS]
        sin_f = forward[turn * height : (turn + 1) * height, COLS:]
        gain = gain_ref[turn + first_det]
        gain_main, gain_zero = gain[:half], gain[half:]
        slabs.append((cos_f[:half] + sin_f[half : 2 * half]) * gain_main)
        slabs.append((cos_f[half : 2 * half] - sin_f[:half]) * gain_main)
        slabs.append(cos_f[2 * half :] * gain_zero)
        slabs.append(-sin_f[2 * half :] * gain_zero)
    back = dot3(split2(jnp.concatenate(slabs, axis=0)), side)
    height = 2 * half + 32
    slabs = []
    for turn in turns:
        cos_b = back[turn * height : (turn + 1) * height, :COLS]
        sin_b = back[turn * height : (turn + 1) * height, COLS:]
        real_u = cos_b[:half] - sin_b[half : 2 * half]
        imag_u = sin_b[:half] + cos_b[half : 2 * half]
        zero_o = cos_b[2 * half : 2 * half + 16] - sin_b[2 * half + 16 :]
        imag_v = real_u * turn_sin + imag_u * turn_cos
        imag_v = jnp.where(row_index == 0, zero_o[0:1], imag_v)
        slabs.append(jnp.concatenate([real_u * turn_cos - imag_u * turn_sin, imag_v], axis=0))
    result = dot3((l_h[...], l_l[...]), split2(jnp.concatenate(slabs, axis=1)))
    results = [result[:, turn * COLS : (turn + 1) * COLS] for turn in turns]
    for turn in turns:
        for half_index in range(HALVES):
            cols = slice(half_index * LANES, (half_index + 1) * LANES)
            start = half_index * rows * dets + first_det + turn
            stacked[pl.ds(start, rows, stride=dets), :] = results[turn][:, cols]
    if final:
        det_index = lax.broadcasted_iota(jnp.int32, (dets, LANES), 0)
        for lane in range(rows * HALVES):
            start = (lane % HALVES * rows + lane // HALVES) * dets
            here = stacked[start : start + dets, :]
            if first_det > 0:
                here = jnp.where(det_index < first_det, before_ref[start : start + dets, :], here)
            out_ref[:, lane * LANES : (lane + 1) * LANES] = here.astype(bf16)
    for turn, result in enumerate(results):
        det = turn + first_det
        totals[...] += binned(high_ref[det], low_ref[det], result, inverse_ref[det], tall)
    if final:
        per_tile = PIX // LOW
        for tile in range(sky_ref.shape[0]):
            source = order_ref[tile] * per_tile
            for piece in range(per_tile):
                cols = slice(piece * LOW, (piece + 1) * LOW)
                sky_ref[tile : tile + 1, cols] = totals[pl.ds(source + piece, 1), :]
                weight_ref[tile : tile + 1, cols] = totals[pl.ds(tall + source + piece, 1), :]


def swap(x, step, axis):
    size = lax.axis_size(axis)
    return lax.ppermute(x, axis, [(i, i ^ step) for i in range(size)])


def vmem(limit):
    return pltpu.CompilerParams(vmem_limit_bytes=limit * MIB)


def shards(
    detector_data, templates, wafer_of, knee_freq, white_level, tile_id, pixel_id, tile_order
):
    row_count, time_local = detector_data.shape
    wafer_count, modes, _ = templates.shape
    owners, groups = lax.axis_size("tm"), lax.axis_size("det")
    run_len = min(row_count, row_count * groups // wafer_count)
    runs = row_count // run_len
    width = runs * (modes + run_len)
    local_dets = row_count // owners
    full_length = time_local * owners
    rows = full_length // COLS
    pieces = time_local // COLS
    paired = owners & (owners - 1) == 0 and 4 <= owners <= 8 and run_len % (2 * local_dets) == 0
    step_len = min(STEP, time_local)
    smem = pl.BlockSpec(memory_space=pltpu.SMEM)
    whole = pl.BlockSpec(memory_space=pltpu.VMEM)
    anywhere = pl.BlockSpec(memory_space=pl.ANY)

    def template_spec(run):
        return pl.BlockSpec((1, modes, step_len), lambda i, w, run=run: (w[run * run_len], 0, i))

    def by_step(height):
        return pl.BlockSpec((height, step_len), lambda i, w: (0, i))

    if paired:
        got = swap(detector_data, 1, "tm")
    sums, *wide = pl.pallas_call(
        functools.partial(fit_kernel, runs, run_len, paired),
        out_shape=[jax.ShapeDtypeStruct((modes, width), f32)]
        + [jax.ShapeDtypeStruct((runs * modes, time_local), f32)] * paired,
        grid_spec=pltpu.PrefetchScalarGridSpec(
            num_scalar_prefetch=1,
            grid=(time_local // step_len,),
            in_specs=[by_step(row_count)] + [template_spec(run) for run in range(runs)],
            out_specs=[pl.BlockSpec((modes, width), lambda i, w: (0, 0))]
            + [by_step(runs * modes)] * paired,
        ),
        compiler_params=vmem(60),
        name="fit_sums",
    )(wafer_of, detector_data, *[templates] * runs)
    if paired:
        wide = swap(wide[0], 1, "tm")
    if paired:
        terms = [sums] + [swap(sums, step, "tm") for step in range(2, owners, 2)]
        while len(terms) > 1:
            terms = [a + b for a, b in zip(terms[0::2], terms[1::2])]
        sums = [terms[0], swap(terms[0], 1, "tm")]
    else:
        sums = [lax.psum(sums, "tm")]

    chunks = 2 if paired and local_dets % 2 == 0 else 1
    per_chunk = local_dets // chunks
    if paired:
        chips = owners // 2
        blocks_out = [(per_chunk, 2 * pieces, COLS)] * (chunks * chips)
        kernel = functools.partial(paired_kernel, runs, run_len, local_dets, chunks)
        operands = [detector_data, got, wide, templates]
        scratch = pltpu.VMEM((HALVES * pieces * row_count, LANES), f32)
    else:
        blocks_out = [(owners, local_dets, pieces, COLS)]
        kernel = functools.partial(residual_kernel, runs, run_len, owners)
        operands = [detector_data, templates]
        scratch = pltpu.VMEM((HALVES * pieces * row_count, LANES), f32)
    fit_amps, *blocks = pl.pallas_call(
        kernel,
        out_shape=[jax.ShapeDtypeStruct(shape, f32) for shape in [(modes, row_count), *blocks_out]],
        in_specs=[smem] + [whole] * (len(sums) + len(operands)),
        out_specs=[whole] * (1 + len(blocks_out)),
        scratch_shapes=[scratch],
        compiler_params=vmem(32),
        name="residual",
    )(wafer_of, *operands, *sums)

    if paired:
        received = [blocks[chunk * chips : (chunk + 1) * chips] for chunk in range(chunks)]
        for step in range(1, chips):
            received[0][step] = swap(received[0][step], 2 * step, "tm")
    else:
        moved = lax.all_to_all(blocks[0], "tm", split_axis=0, concat_axis=0, tiled=True)
        received = [[jnp.swapaxes(moved, 0, 1).reshape(local_dets, rows, COLS)]]

    tile_count = tile_order.shape[0]
    tall = tile_count * PIX // LOW
    table = jnp.asarray(tables(rows))
    half = rows // 2
    grid_shape = (local_dets, rows, COLS)
    pair_shapes = [(rows, rows), (COLS, 2 * COLS), (rows, rows)]
    pairs = [jax.ShapeDtypeStruct(shape, bf16) for shape in pair_shapes for _ in range(2)]
    prepared_shapes = [
        (half, COLS),
        (half, COLS),
        (local_dets, half + 16, COLS),
        (local_dets, 1, COLS),
        grid_shape,
        grid_shape,
    ]
    prepared = pl.pallas_call(
        prepare_kernel,
        out_shape=pairs + [jax.ShapeDtypeStruct(shape, f32) for shape in prepared_shapes],
        in_specs=[smem, smem, anywhere, whole, whole, whole],
        out_specs=[whole] * 12,
        scratch_shapes=[pltpu.VMEM((HALVES * rows * local_dets, LANES), f32)] * 2,
        compiler_params=vmem(32),
        cost_estimate=pl.CostEstimate(
            flops=0, bytes_accessed=32 * local_dets * full_length, transcendentals=0
        ),
        name="prepare",
    )(knee_freq, white_level, fit_amps, table, tile_id, pixel_id)

    for chunk in range(1, chunks):
        near = [received[chunk - 1][2:3], received[chunk], prepared]
        near = lax.optimization_barrier(near)
        received[chunk - 1][2:3], received[chunk], prepared = near
        for step in range(1, chips):
            received[chunk][step] = swap(received[chunk][step], 2 * step, "tm")

    stacked_shape = (HALVES * rows * local_dets, LANES)
    carried = []
    for chunk in range(chunks):
        final = chunk == chunks - 1
        first_det = chunk * per_chunk
        parts = len(received[chunk])
        if final:
            outs = [((local_dets, full_length), bf16)] + [((tile_count, PIX), f32)] * 2
            scratch = [pltpu.VMEM(s, f32) for s in ((rows, per_chunk * COLS), stacked_shape, (2 * tall, LOW))]
        else:
            outs = [(stacked_shape, f32), ((2 * tall, LOW), f32)]
            scratch = [pltpu.VMEM((rows, per_chunk * COLS), f32)]
        operands = [*received[chunk], *prepared, *carried]
        carried = pl.pallas_call(
            functools.partial(filter_kernel, parts, first_det, per_chunk, local_dets, final),
            out_shape=[jax.ShapeDtypeStruct(*o) for o in outs],
            in_specs=[smem] + [whole] * len(operands),
            out_specs=[whole] * len(outs),
            scratch_shapes=scratch,
            compiler_params=vmem(32),
            cost_estimate=pl.CostEstimate(
                flops=80000 * per_chunk * full_length,
                bytes_accessed=16 * per_chunk * full_length,
                transcendentals=0,
            ),
            name="filter_and_bin",
        )(tile_order, *operands)
    weighted_data, sky_part, weight_part = carried

    owned = tile_count * PIX // owners
    both = jnp.concatenate(
        [sky_part.reshape(owners, owned), weight_part.reshape(owners, owned)], axis=1
    )
    spread = jnp.broadcast_to(both[None], (groups, *both.shape)).reshape(groups * owners, 2 * owned)
    spread = lax.all_to_all(spread, ("det", "tm"), split_axis=0, concat_axis=0, tiled=True)
    scale = float(tile_count * PIX) / float(local_dets * groups * owners * full_length)
    summed = jnp.sum(spread, axis=0) * scale
    return (fit_amps, weighted_data, summed[:owned], summed[owned:])


def solution(mesh):
    in_specs = (
        P("det", "tm"),
        P(None, None, "tm"),
        P("det"),
        P(("det", "tm")),
        P(("det", "tm")),
        P(("det", "tm"), None),
        P(("det", "tm"), None),
        P(),
    )
    out_specs = (P(None, "det"), P(("det", "tm"), None), P("tm"), P("tm"))
    return jax.shard_map(shards, mesh=mesh, in_specs=in_specs, out_specs=out_specs, check_vma=False)
```

```python
import functools
import math

import jax
import jax.numpy as jnp
import numpy as np
from jax import lax
from jax.experimental import pallas as pl
from jax.experimental.pallas import tpu as pltpu
from jax.sharding import PartitionSpec as P

PIX = 128
COLS = 256
LANES = 128
HALVES = COLS // LANES
LOW = 64
SAMPLE_RATE = 200.0
MIB = 1024 * 1024
STEP = 8192
NT = (((1,), (1,)), ((), ()))
f32 = jnp.float32
bf16 = jnp.bfloat16


def split2(x):
    high = x.astype(bf16)
    return high, (x - high.astype(f32)).astype(bf16)


def split3(x):
    high = x.astype(bf16)
    rest = x - high.astype(f32)
    mid = rest.astype(bf16)
    return high, mid, (rest - mid.astype(f32)).astype(bf16)


@functools.lru_cache(maxsize=None)
def tables(rows):
    total = rows * COLS
    half = rows // 2
    slots = np.arange(half)
    slots[0] = half
    ramp = np.arange(rows)
    angle = 2.0 * np.pi * (slots[:, None] * ramp[None, :] % rows) / rows
    first = np.concatenate([np.cos(angle), -np.sin(angle)], axis=0)
    first[half] = 1.0
    weight = np.full((half,), 2.0)
    weight[0] = 1.0
    last = np.concatenate([weight[:, None] * np.cos(angle), -2.0 * np.sin(angle)], axis=0)
    last[half] = 1.0
    last = last.T / total
    col = np.arange(COLS)
    phase = 2.0 * np.pi * (col[:, None] * col[None, :] % COLS) / COLS
    turn = 2.0 * np.pi * (slots[:, None] * col[None, :] % total) / total
    bins = np.concatenate([slots, np.zeros((16,), np.int64)])[:, None] + rows * col[None, :]
    freq = np.minimum(bins, total - bins).astype(np.float32) * np.float32(SAMPLE_RATE / total)
    made = [first, np.cos(phase), np.sin(phase), last, np.cos(turn), np.sin(turn), freq * freq]
    return np.concatenate([table.astype(np.float32) for table in made], axis=0)


def dot3(left, right):
    (lh, ll), (rh, rl) = left, right
    return jnp.dot(
        jnp.concatenate([lh, ll, lh], axis=1),
        jnp.concatenate([rh, rh, rl], axis=0),
        preferred_element_type=f32,
    )


def fit_kernel(runs, run_len, paired, wafer_ref, data_ref, *refs):
    template_refs, out_ref = refs[:runs], refs[runs]
    parts = []
    for run in range(runs):
        temp = template_refs[run][0]
        modes = temp.shape[0]
        high, mid, low = split3(data_ref[run * run_len : (run + 1) * run_len, :])
        both = lax.dot_general(
            temp, jnp.concatenate([temp, high, mid, low], axis=0), NT, preferred_element_type=f32
        )
        ends = [modes + i * run_len for i in range(4)]
        parts.append(both[:, :modes])
        parts.append(
            both[:, ends[0] : ends[1]] + both[:, ends[1] : ends[2]] + both[:, ends[2] : ends[3]]
        )
        if paired:
            refs[runs + 1][run * modes : (run + 1) * modes, :] = temp.astype(f32)
    part = jnp.concatenate(parts, axis=1)

    @pl.when(pl.program_id(0) == 0)
    def _():
        out_ref[...] = part

    @pl.when(pl.program_id(0) > 0)
    def _():
        out_ref[...] += part


def eliminate(sums, runs, run_len, modes):
    width = modes + run_len
    row_index = lax.broadcasted_iota(jnp.int32, (modes, width), 0)
    joined = [sums[:, run * width : (run + 1) * width] for run in range(runs)]
    for column in range(modes):
        for run in range(runs):
            now = joined[run]
            factor = jnp.broadcast_to(now[:, column : column + 1], now.shape)
            pivot_row = now[column : column + 1, :] / factor[column : column + 1, :]
            rest = now - factor * pivot_row
            joined[run] = jnp.where(row_index == column, pivot_row, rest)
    return [now[:, modes:] for now in joined]


def paired_kernel(
    runs, run_len, local_dets, chunks, wafer_ref, data_ref, got_ref, wide_ref, temp_ref, *refs
):
    chips = data_ref.shape[0] // (2 * local_dets)
    sums, refs = refs[0][...] + refs[1][...], refs[2:]
    amps_ref, out_refs, rows_ref = refs[0], refs[1:-1], refs[-1]
    modes = temp_ref.shape[1]
    row_count, time_local = data_ref.shape
    kept = row_count // 2
    pieces = time_local // COLS
    amps = eliminate(sums, runs, run_len, modes)
    amps_ref[...] = jnp.concatenate(amps, axis=1)
    me = lax.axis_index("tm")
    core, chip = jnp.bitwise_and(me, 1), jnp.right_shift(me, 1)
    per_run = run_len // 2
    shard_rows = HALVES * pieces * kept

    def mine(rows):
        groups = [rows[start : start + local_dets] for start in range(0, run_len, local_dets)]
        even, odd = jnp.concatenate(groups[0::2], axis=0), jnp.concatenate(groups[1::2], axis=0)
        return jnp.where(core == 0, even, odd)

    for run in range(runs):
        left = jnp.concatenate(split3(mine(amps[run].T)), axis=1)
        own = temp_ref[wafer_ref[run * run_len]]
        other = wide_ref[run * modes : (run + 1) * modes, :].astype(bf16)
        for side, (temp, source) in enumerate([(own, data_ref), (other, got_ref)]):
            fitted = jnp.dot(left, jnp.concatenate([temp] * 3, axis=0), preferred_element_type=f32)
            kept_rows = mine(source[run * run_len : (run + 1) * run_len, :]) - fitted
            for lane in range(time_local // LANES):
                start = side * shard_rows + run * per_run
                start += (lane % HALVES * pieces + lane // HALVES) * kept
                rows_ref[start : start + per_run, :] = kept_rows[:, lane * LANES : (lane + 1) * LANES]
    per_chunk = local_dets // chunks
    for chunk in range(chunks):
        for step in range(chips):
            base = jnp.bitwise_xor(chip, step) * local_dets + chunk * per_chunk
            for det in range(per_chunk):
                for side in range(2):
                    place = pl.multiple_of(jnp.bitwise_xor(core, side) * pieces, pieces)
                    out_refs[chunk * chips + step][det, pl.ds(place, pieces), :] = take_rows(
                        rows_ref, side * shard_rows + base + det, pieces, kept
                    )


def residual_kernel(runs, run_len, owners, wafer_ref, data_ref, temp_ref, sums_ref, *refs):
    amps_ref, out_ref, rows_ref = refs
    modes = temp_ref.shape[1]
    row_count, time_local = data_ref.shape
    pieces = time_local // COLS
    amps = eliminate(sums_ref[...], runs, run_len, modes)
    amps_ref[...] = jnp.concatenate(amps, axis=1)
    for run in range(runs):
        temp = temp_ref[wafer_ref[run * run_len]]
        left = jnp.concatenate(split3(amps[run].T), axis=1)
        fitted = jnp.dot(left, jnp.concatenate([temp] * 3, axis=0), preferred_element_type=f32)
        rows = slice(run * run_len, (run + 1) * run_len)
        for lane in range(time_local // LANES):
            cols = slice(lane * LANES, (lane + 1) * LANES)
            start = (lane % HALVES * pieces + lane // HALVES) * row_count + run * run_len
            rows_ref[start : start + run_len, :] = data_ref[rows, cols] - fitted[:, cols]
    local_dets = row_count // owners
    for owner in range(owners):
        for det in range(local_dets):
            out_ref[owner, det] = take_rows(rows_ref, owner * local_dets + det, pieces, row_count)


def take_rows(ref, start, count, stride):
    return jnp.concatenate(
        [
            ref[pl.ds(side * count * stride + start, count, stride=stride), :]
            for side in range(HALVES)
        ],
        axis=1,
    )


def binned(high_rows, low_rows, value_rows, weight_row, tall):
    high_ramp = lax.broadcasted_iota(jnp.int32, (tall, COLS), 0).astype(f32).astype(bf16)
    low_ramp = lax.broadcasted_iota(jnp.int32, (LOW, COLS), 0).astype(f32).astype(bf16)
    weight = jnp.broadcast_to(weight_row, (tall, COLS)).astype(bf16)
    zero, one = jnp.zeros((tall, COLS), bf16), jnp.ones((LOW, COLS), bf16)
    lefts, rights = [], []
    for row in range(high_rows.shape[0]):
        high = jnp.broadcast_to(high_rows[row : row + 1], (tall, COLS)).astype(bf16)
        low = jnp.broadcast_to(low_rows[row : row + 1], (LOW, COLS)).astype(bf16)
        value = jnp.broadcast_to(value_rows[row : row + 1], (tall, COLS)).astype(bf16)
        hot = high == high_ramp
        lefts.append(
            jnp.concatenate([jnp.where(hot, value, zero), jnp.where(hot, weight, zero)], axis=0)
        )
        rights.append(jnp.where(low == low_ramp, one, jnp.zeros_like(one)))
    return lax.dot_general(
        jnp.concatenate(lefts, axis=1),
        jnp.concatenate(rights, axis=1),
        NT,
        preferred_element_type=f32,
    )


def prepare_kernel(knee_ref, white_ref, after_ref, table_ref, tile_ref, pixel_ref, *refs):
    outs, (turn_cos, turn_sin, gain_ref, inverse_ref, high_ref, low_ref, hi_s, lo_s) = refs[:6], refs[6:]
    local_dets, rows = high_ref.shape[0], high_ref.shape[1]
    half = rows // 2
    tables_at = [0]
    for height in (rows, COLS, COLS, rows, half, half):
        tables_at.append(tables_at[-1] + height)
    first, cosine, sine, last, turn_c, turn_s = (
        table_ref[start:end, :] for start, end in zip(tables_at[:-1], tables_at[1:])
    )
    for i, table in enumerate((first, jnp.concatenate([cosine, sine], axis=1), last)):
        outs[2 * i][...], outs[2 * i + 1][...] = split2(table)
    turn_cos[...], turn_sin[...] = turn_c, turn_s
    squared = table_ref[tables_at[-1] :, :]
    cell = tile_ref[...] * PIX + pixel_ref[...]
    high = jnp.right_shift(cell, LOW.bit_length() - 1).astype(f32)
    low = jnp.bitwise_and(cell, LOW - 1).astype(f32)
    for lane in range(rows * HALVES):
        cols = slice(lane * LANES, (lane + 1) * LANES)
        start = (lane % HALVES * rows + lane // HALVES) * local_dets
        hi_s[start : start + local_dets, :] = high[:, cols]
        lo_s[start : start + local_dets, :] = low[:, cols]
    for det in range(local_dets):
        high_ref[det] = take_rows(hi_s, det, rows, local_dets)
        low_ref[det] = take_rows(lo_s, det, rows, local_dets)
        knee = knee_ref[det]
        gain_ref[det] = squared / (white_ref[det] * (squared + knee * knee))
        inverse_ref[det] = 1.0 / jnp.full((1, COLS), white_ref[det], f32)


def filter_kernel(parts, first_det, count, dets, final, order_ref, *refs):
    part_refs = refs[:parts]
    (f_h, f_l, s_h, s_l, l_h, l_l, tc_ref, ts_ref, gain_ref, inverse_ref, high_ref, low_ref) = refs[
        parts : parts + 12
    ]
    refs = refs[parts + 12 :]
    if first_det > 0:
        before_ref, sums_ref, refs = refs[0], refs[1], refs[2:]
    if final:
        out_ref, sky_ref, weight_ref, signal, stacked, totals = refs
    else:
        stacked, totals, signal = refs
    rows = signal.shape[0]
    half = rows // 2
    totals[...] = sums_ref[...] if first_det > 0 else jnp.zeros_like(totals)
    tall = totals.shape[0] // 2
    row_index = lax.broadcasted_iota(jnp.int32, (half, COLS), 0)
    chip = jnp.right_shift(lax.axis_index("tm"), 1)

    turn_cos, turn_sin = tc_ref[...], ts_ref[...]
    side = (s_h[...], s_l[...])
    turns = range(count)
    slabs = []
    for turn in turns:
        for part in range(parts):
            height = part_refs[part].shape[1]
            start = 0
            if parts > 1:
                start = pl.multiple_of(jnp.bitwise_xor(chip, part) * height, height)
            signal[pl.ds(start, height), turn * COLS : (turn + 1) * COLS] = part_refs[part][turn]
    first = dot3((f_h[...], f_l[...]), split2(signal[...]))
    for turn in turns:
        cols = slice(turn * COLS, (turn + 1) * COLS)
        real_y, low_y = first[:half, cols], first[half:, cols]
        imag_y = jnp.where(row_index == 0, 0.0, low_y)
        slabs.append(real_y * turn_cos + imag_y * turn_sin)
        slabs.append(imag_y * turn_cos - real_y * turn_sin)
        slabs.append(jnp.broadcast_to(low_y[0:1], (16, COLS)))
    forward = dot3(split2(jnp.concatenate(slabs, axis=0)), side)
    height = 2 * half + 16
    slabs = []
    for turn in turns:
        cos_f = forward[turn * height : (turn + 1) * height, :COLS]
        sin_f = forward[turn * height : (turn + 1) * height, COLS:]
        gain = gain_ref[turn + first_det]
        gain_main, gain_zero = gain[:half], gain[half:]
        slabs.append((cos_f[:half] + sin_f[half : 2 * half]) * gain_main)
        slabs.append((cos_f[half : 2 * half] - sin_f[:half]) * gain_main)
        slabs.append(cos_f[2 * half :] * gain_zero)
        slabs.append(-sin_f[2 * half :] * gain_zero)
    back = dot3(split2(jnp.concatenate(slabs, axis=0)), side)
    height = 2 * half + 32
    slabs = []
    for turn in turns:
        cos_b = back[turn * height : (turn + 1) * height, :COLS]
        sin_b = back[turn * height : (turn + 1) * height, COLS:]
        real_u = cos_b[:half] - sin_b[half : 2 * half]
        imag_u = sin_b[:half] + cos_b[half : 2 * half]
        zero_o = cos_b[2 * half : 2 * half + 16] - sin_b[2 * half + 16 :]
        imag_v = real_u * turn_sin + imag_u * turn_cos
        imag_v = jnp.where(row_index == 0, zero_o[0:1], imag_v)
        slabs.append(jnp.concatenate([real_u * turn_cos - imag_u * turn_sin, imag_v], axis=0))
    result = dot3((l_h[...], l_l[...]), split2(jnp.concatenate(slabs, axis=1)))
    results = [result[:, turn * COLS : (turn + 1) * COLS] for turn in turns]
    for turn in turns:
        for half_index in range(HALVES):
            cols = slice(half_index * LANES, (half_index + 1) * LANES)
            start = half_index * rows * dets + first_det + turn
            stacked[pl.ds(start, rows, stride=dets), :] = results[turn][:, cols]
    if final:
        det_index = lax.broadcasted_iota(jnp.int32, (dets, LANES), 0)
        for lane in range(rows * HALVES):
            start = (lane % HALVES * rows + lane // HALVES) * dets
            here = stacked[start : start + dets, :]
            if first_det > 0:
                here = jnp.where(det_index < first_det, before_ref[start : start + dets, :], here)
            out_ref[:, lane * LANES : (lane + 1) * LANES] = here.astype(bf16)
    for turn, result in enumerate(results):
        det = turn + first_det
        totals[...] += binned(high_ref[det], low_ref[det], result, inverse_ref[det], tall)
    if final:
        per_tile = PIX // LOW
        for tile in range(sky_ref.shape[0]):
            source = order_ref[tile] * per_tile
            for piece in range(per_tile):
                cols = slice(piece * LOW, (piece + 1) * LOW)
                sky_ref[tile : tile + 1, cols] = totals[pl.ds(source + piece, 1), :]
                weight_ref[tile : tile + 1, cols] = totals[pl.ds(tall + source + piece, 1), :]


def swap(x, step, axis):
    size = lax.axis_size(axis)
    return lax.ppermute(x, axis, [(i, i ^ step) for i in range(size)])


def vmem(limit):
    return pltpu.CompilerParams(vmem_limit_bytes=limit * MIB)


def shards(
    detector_data, templates, wafer_of, knee_freq, white_level, tile_id, pixel_id, tile_order
):
    row_count, time_local = detector_data.shape
    wafer_count, modes, _ = templates.shape
    owners, groups = lax.axis_size("tm"), lax.axis_size("det")
    run_len = min(row_count, row_count * groups // wafer_count)
    runs = row_count // run_len
    width = runs * (modes + run_len)
    local_dets = row_count // owners
    full_length = time_local * owners
    rows = full_length // COLS
    pieces = time_local // COLS
    paired = owners & (owners - 1) == 0 and 4 <= owners <= 8 and run_len % (2 * local_dets) == 0
    step_len = min(STEP, time_local)
    smem = pl.BlockSpec(memory_space=pltpu.SMEM)
    whole = pl.BlockSpec(memory_space=pltpu.VMEM)
    anywhere = pl.BlockSpec(memory_space=pl.ANY)

    def template_spec(run):
        return pl.BlockSpec((1, modes, step_len), lambda i, w, run=run: (w[run * run_len], 0, i))

    def by_step(height):
        return pl.BlockSpec((height, step_len), lambda i, w: (0, i))

    if paired:
        got = swap(detector_data, 1, "tm")
    sums, *wide = pl.pallas_call(
        functools.partial(fit_kernel, runs, run_len, paired),
        out_shape=[jax.ShapeDtypeStruct((modes, width), f32)]
        + [jax.ShapeDtypeStruct((runs * modes, time_local), f32)] * paired,
        grid_spec=pltpu.PrefetchScalarGridSpec(
            num_scalar_prefetch=1,
            grid=(time_local // step_len,),
            in_specs=[by_step(row_count)] + [template_spec(run) for run in range(runs)],
            out_specs=[pl.BlockSpec((modes, width), lambda i, w: (0, 0))]
            + [by_step(runs * modes)] * paired,
        ),
        compiler_params=vmem(60),
        name="fit_sums",
    )(wafer_of, detector_data, *[templates] * runs)
    if paired:
        wide = swap(wide[0], 1, "tm")
    if paired:
        terms = [sums] + [swap(sums, step, "tm") for step in range(2, owners, 2)]
        while len(terms) > 1:
            terms = [a + b for a, b in zip(terms[0::2], terms[1::2])]
        sums = [terms[0], swap(terms[0], 1, "tm")]
    else:
        sums = [lax.psum(sums, "tm")]

    chunks = 2 if paired and local_dets % 2 == 0 else 1
    per_chunk = local_dets // chunks
    if paired:
        chips = owners // 2
        blocks_out = [(per_chunk, 2 * pieces, COLS)] * (chunks * chips)
        kernel = functools.partial(paired_kernel, runs, run_len, local_dets, chunks)
        operands = [detector_data, got, wide, templates]
        scratch = pltpu.VMEM((HALVES * pieces * row_count, LANES), f32)
    else:
        blocks_out = [(owners, local_dets, pieces, COLS)]
        kernel = functools.partial(residual_kernel, runs, run_len, owners)
        operands = [detector_data, templates]
        scratch = pltpu.VMEM((HALVES * pieces * row_count, LANES), f32)
    fit_amps, *blocks = pl.pallas_call(
        kernel,
        out_shape=[jax.ShapeDtypeStruct(shape, f32) for shape in [(modes, row_count), *blocks_out]],
        in_specs=[smem] + [whole] * (len(sums) + len(operands)),
        out_specs=[whole] * (1 + len(blocks_out)),
        scratch_shapes=[scratch],
        compiler_params=vmem(32),
        name="residual",
    )(wafer_of, *operands, *sums)

    if paired:
        received = [blocks[chunk * chips : (chunk + 1) * chips] for chunk in range(chunks)]
        for step in range(1, chips):
            received[0][step] = swap(received[0][step], 2 * step, "tm")
    else:
        moved = lax.all_to_all(blocks[0], "tm", split_axis=0, concat_axis=0, tiled=True)
        received = [[jnp.swapaxes(moved, 0, 1).reshape(local_dets, rows, COLS)]]

    tile_count = tile_order.shape[0]
    tall = tile_count * PIX // LOW
    table = jnp.asarray(tables(rows))
    half = rows // 2
    grid_shape = (local_dets, rows, COLS)
    pair_shapes = [(rows, rows), (COLS, 2 * COLS), (rows, rows)]
    pairs = [jax.ShapeDtypeStruct(shape, bf16) for shape in pair_shapes for _ in range(2)]
    prepared_shapes = [
        (half, COLS),
        (half, COLS),
        (local_dets, half + 16, COLS),
        (local_dets, 1, COLS),
        grid_shape,
        grid_shape,
    ]
    prepared = pl.pallas_call(
        prepare_kernel,
        out_shape=pairs + [jax.ShapeDtypeStruct(shape, f32) for shape in prepared_shapes],
        in_specs=[smem, smem, anywhere, whole, whole, whole],
        out_specs=[whole] * 12,
        scratch_shapes=[pltpu.VMEM((HALVES * rows * local_dets, LANES), f32)] * 2,
        compiler_params=vmem(32),
        cost_estimate=pl.CostEstimate(
            flops=0, bytes_accessed=32 * local_dets * full_length, transcendentals=0
        ),
        name="prepare",
    )(knee_freq, white_level, fit_amps, table, tile_id, pixel_id)

    for chunk in range(1, chunks):
        near = [received[chunk - 1][2:3], received[chunk], prepared]
        near = lax.optimization_barrier(near)
        received[chunk - 1][2:3], received[chunk], prepared = near
        for step in range(1, chips):
            received[chunk][step] = swap(received[chunk][step], 2 * step, "tm")

    stacked_shape = (HALVES * rows * local_dets, LANES)
    carried = []
    for chunk in range(chunks):
        final = chunk == chunks - 1
        first_det = chunk * per_chunk
        parts = len(received[chunk])
        if final:
            outs = [((local_dets, full_length), bf16)] + [((tile_count, PIX), f32)] * 2
            scratch = [pltpu.VMEM(s, f32) for s in ((rows, per_chunk * COLS), stacked_shape, (2 * tall, LOW))]
        else:
            outs = [(stacked_shape, f32), ((2 * tall, LOW), f32)]
            scratch = [pltpu.VMEM((rows, per_chunk * COLS), f32)]
        operands = [*received[chunk], *prepared, *carried]
        carried = pl.pallas_call(
            functools.partial(filter_kernel, parts, first_det, per_chunk, local_dets, final),
            out_shape=[jax.ShapeDtypeStruct(*o) for o in outs],
            in_specs=[smem] + [whole] * len(operands),
            out_specs=[whole] * len(outs),
            scratch_shapes=scratch,
            compiler_params=vmem(32),
            cost_estimate=pl.CostEstimate(
                flops=80000 * per_chunk * full_length,
                bytes_accessed=16 * per_chunk * full_length,
                transcendentals=0,
            ),
            name="filter_and_bin",
        )(tile_order, *operands)
    weighted_data, sky_part, weight_part = carried

    owned = tile_count * PIX // owners
    both = jnp.concatenate(
        [sky_part.reshape(owners, owned), weight_part.reshape(owners, owned)], axis=1
    )
    spread = jnp.broadcast_to(both[None], (groups, *both.shape)).reshape(groups * owners, 2 * owned)
    spread = lax.all_to_all(spread, ("det", "tm"), split_axis=0, concat_axis=0, tiled=True)
    scale = float(tile_count * PIX) / float(local_dets * groups * owners * full_length)
    summed = jnp.sum(spread, axis=0) * scale
    return (fit_amps, weighted_data, summed[:owned], summed[owned:])


def solution(mesh):
    in_specs = (
        P("det", "tm"),
        P(None, None, "tm"),
        P("det"),
        P(("det", "tm")),
        P(("det", "tm")),
        P(("det", "tm"), None),
        P(("det", "tm"), None),
        P(),
    )
    out_specs = (P(None, "det"), P(("det", "tm"), None), P("tm"), P("tm"))
    return jax.shard_map(shards, mesh=mesh, in_specs=in_specs, out_specs=out_specs, check_vma=False)
```
